32 devices in a mesh: dp: 16 (over z, y, core), tensor: 2 (over x).
Axes of the slice: x: 2, y: 2, z: 4, core: 2. Of those that a mesh axis runs over, the one named last changes fastest.
Arguments:
- hidden_in: bfloat16 [16384, 8192], P(('dp', 'tensor')), parts along dimension 0, may hold values from -6 to 6
- queries: bfloat16 [16384, 4096], P('dp', 'tensor'), parts along dimension 0, may hold values from -104 to 104
- keys: bfloat16 [16384, 1024], P('dp', 'tensor'), parts along dimension 0, may hold values from -4 to 4
- values: bfloat16 [16384, 1024], P('dp', 'tensor'), parts along dimension 0, may hold values from -6 to 6
- out_grad: bfloat16 [16384, 4096], P('dp', 'tensor'), parts along dimension 0, may hold values from -6 to 6
- key_weight: bfloat16 [8192, 1024], P(None, 'tensor'), may hold values from -0.0625 to 0.0625
- value_weight: bfloat16 [8192, 1024], P(None, 'tensor'), may hold values from -0.0625 to 0.0625
- in_basis: bfloat16 [8192, 64], replicated, may hold values from -0.0625 to 0.0625
- key_basis: bfloat16 [1024, 64], P('tensor'), may hold values from -0.1875 to 0.1875
- value_basis: bfloat16 [1024, 64], P('tensor'), may hold values from -0.1875 to 0.1875
- doc_ids: int32 [16384], P('dp'), parts along dimension 0, may hold values from 0 to 7, never falling along the last dimension, each value on 1 to 256 neighbouring positions
Outputs:
- input_grad: bfloat16 [16384, 8192], P(('dp', 'tensor')), parts along dimension 0
- key_docs: float32 [128, 64, 64], P(('dp', 'tensor')), parts along dimension 0
- value_docs: float32 [128, 64, 64], P(('dp', 'tensor')), parts along dimension 0
The draws below stay inside these ranges and needn't reach their ends.
There are 16 independent parts, one for each index of `dp`. The reference program is written for one: setup_inputs(seed, part) draws one part's arguments, and reference() takes and returns one part's arrays. A program takes and returns all parts, laid end to end along the dimension named above; an argument that names none is the same for every part. Nothing has to cross between parts.
Inputs may be any that keep to these rules, and one draw needn't show every extreme that they name: `doc_ids`: never falling along the tokens; each document holds 1 to 256 tokens and one holds exactly 256.
All inputs are finite; a program needn't handle non-finite values.
Results may differ from the reference program's by a relative error of at most 0.013.
Values may be sent and summed in bfloat16 or wider, within the bound.
No kernel may reach another device: no remote copies, remote signals or barrier semaphores. Data moves between devices by JAX's collectives and lax.ppermute only.
A program may use at most 256 MiB of HBM per device.

```python
import math
import jax
import jax.numpy as jnp
import numpy as np
from jax import lax

D = 8192
KV = 8
HD = 128
QH = 32
RANK = 64
DOCS = 8
TOK = 1024
MOST = 256
N_TENSOR = 2


def base_keys(key):
    return jnp.clip(jax.random.normal(key, (TOK, KV * HD), jnp.float32), -4.0, 4.0)


def draw_keys(key, part):
    base = base_keys(key)
    return base.astype(jnp.bfloat16)


def draw_queries(key, part):
    key = jax.random.fold_in(key, 5)
    fresh = jnp.clip(jax.random.normal(key, (TOK, QH * HD), jnp.float32), -4.0, 4.0)
    return fresh.astype(jnp.bfloat16)


def steps_of(stream_key, extent, cuts, smallest, high):
    def one(dim, shards_of):
        steps = jax.random.uniform(jax.random.fold_in(jax.random.fold_in(stream_key, 6), dim), (shards_of,), jnp.float32, smallest / len(cuts), high / len(cuts))
        return jnp.repeat(jnp.exp(steps), extent[dim] // shards_of).reshape((-1,) + (1,) * (len(extent) - dim - 1))

    loudness = one(*cuts[0])
    for cut in cuts[1:]:
        loudness = loudness * one(*cut)
    return loudness


def length_profile(amount, total, reach, skew):
    weights = [(1 << 20) // math.isqrt(grade ** skew) + 1 for grade in range(2, amount + 1)]
    spare, counts = total - reach - (amount - 1), [1] * (amount - 1)
    while spare > 0:
        free = [i for i in range(amount - 1) if counts[i] < reach]
        mass, remaining = sum([weights[i] for i in free]), spare
        for i in free:
            more = min(reach - counts[i], max(1, remaining * weights[i] // mass), spare)
            counts[i] = counts[i] + more
            spare = spare - more
    return np.array([reach] + counts)


def ragged(key, amount, total, most, slope):
    if amount == 2:
        one = jax.random.randint(key, (), max(1, total - most), min(most, total - 1) + 1)
        return jnp.stack([one, total - one])
    sizes = jnp.asarray(length_profile(amount, total, most, slope), jnp.int32)
    couples = (amount - 1) // 2
    giver, taker = sizes[1:1 + 2 * couples:2], sizes[2:2 + 2 * couples:2]
    slack = jnp.minimum(giver - 1, most - taker)
    passed = jax.random.randint(jax.random.fold_in(key, 1), (couples,), 0, 1 << 20) % (slack + 1)
    sizes = sizes.at[1:1 + 2 * couples:2].set(giver - passed).at[2:2 + 2 * couples:2].set(taker + passed)
    return sizes[jax.random.permutation(jax.random.fold_in(key, 2), amount)]


def scatter_about(key, dims, scale, limit, cuts=(), kind=jnp.bfloat16):
    level = steps_of(key, dims, cuts, -0.22, 0.18) if cuts else 1.0
    result = jax.random.normal(key, dims, jnp.float32) * scale * level
    return jnp.minimum(jnp.maximum(result, -limit), limit).astype(kind)


def setup_inputs(seed: int = 0, part: int = 0) -> dict:
    key_list = jax.random.split(jax.random.key(seed), 12)
    own_keys = jax.random.split(jax.random.fold_in(key_list[11], part), 12)
    return {
        "hidden_in": scatter_about(own_keys[0], (TOK, D), 1.0, 6.0, ((0, 2),)),
        "queries": draw_queries(jax.random.fold_in(jax.random.fold_in(key_list[11], part), 71), part),
        "keys": draw_keys(jax.random.fold_in(jax.random.fold_in(key_list[11], part), 71), part),
        "values": scatter_about(own_keys[3], (TOK, KV * HD), 1.0, 6.0, ((1, 2),)),
        "out_grad": scatter_about(own_keys[4], (TOK, QH * HD), 1.0, 6.0, ((1, 2),)),
        "key_weight": scatter_about(key_list[5], (D, KV * HD), D ** -0.5, 0.0625, ((1, 2),)),
        "value_weight": scatter_about(key_list[6], (D, KV * HD), D ** -0.5, 0.0625, ((1, 2),)),
        "in_basis": scatter_about(key_list[7], (D, RANK), D ** -0.5, 0.0625),
        "key_basis": scatter_about(key_list[8], (KV * HD, RANK), (KV * HD) ** -0.5, 0.1875, ((0, 2),)),
        "value_basis": scatter_about(key_list[9], (KV * HD, RANK), (KV * HD) ** -0.5, 0.1875, ((0, 2),)),
        "doc_ids": jnp.searchsorted(jnp.cumsum(ragged(own_keys[10], DOCS, TOK, MOST, 1)), jnp.arange(TOK), side="right").astype(jnp.int32),
    }


def allowed_pairs(doc_ids):
    count = doc_ids.shape[0]
    position = jnp.arange(count, dtype=jnp.int32)
    same_doc = doc_ids[:, None] == doc_ids[None, :]
    return same_doc & (position[None, :] <= position[:, None])


def group_grads(query_heads, key_head, value_head, grad_heads, allowed):
    scale = HD ** -0.5

    def one_head(carry, operands):
        query, grad_out = operands
        scores = jnp.dot(query, key_head.T, preferred_element_type=jnp.float32) * scale
        scores = jnp.where(allowed, scores, -1e30)
        peak = jnp.max(scores, axis=1, keepdims=True)
        expo = jnp.exp(scores - peak)
        probs = expo / jnp.sum(expo, axis=1, keepdims=True)
        probs_low = probs.astype(jnp.bfloat16)
        value_step = lax.dot_general(probs_low, grad_out, (((0,), (0,)), ((), ())), preferred_element_type=jnp.float32)
        dprobs = jnp.dot(grad_out, value_head.T, preferred_element_type=jnp.float32)
        delta = jnp.sum(probs * dprobs, axis=1, keepdims=True)
        dscores = (probs * (dprobs - delta)).astype(jnp.bfloat16)
        key_step = lax.dot_general(dscores, query, (((0,), (0,)), ((), ())), preferred_element_type=jnp.float32) * scale
        return (carry[0] + key_step, carry[1] + value_step), None

    zeros = jnp.zeros((query_heads.shape[1], query_heads.shape[2]), jnp.float32)
    (key_sum, value_sum), _ = lax.scan(one_head, (zeros, zeros), (query_heads, grad_heads))
    return key_sum.astype(jnp.bfloat16), value_sum.astype(jnp.bfloat16)


def doc_outer(weighted, grads):
    return lax.dot_general(weighted, grads, (((0,), (0,)), ((), ())), precision=lax.Precision.HIGHEST, preferred_element_type=jnp.float32)


def reference(hidden_in, queries, keys, values, out_grad, key_weight, value_weight, in_basis, key_basis, value_basis, doc_ids):
    group = QH // KV
    allowed = allowed_pairs(doc_ids)
    query_heads = queries.reshape(TOK, KV, group, HD).transpose(1, 2, 0, 3)
    grad_heads = out_grad.reshape(TOK, KV, group, HD).transpose(1, 2, 0, 3)
    key_heads = keys.reshape(TOK, KV, HD).transpose(1, 0, 2)
    value_heads = values.reshape(TOK, KV, HD).transpose(1, 0, 2)
    key_grad, value_grad = lax.map(lambda ops: group_grads(ops[0], ops[1], ops[2], ops[3], allowed), (query_heads, key_heads, value_heads, grad_heads))
    local_kv = KV // N_TENSOR
    key_blocks = key_grad.reshape(N_TENSOR, local_kv, TOK, HD)
    value_blocks = value_grad.reshape(N_TENSOR, local_kv, TOK, HD)
    weight_keys = key_weight.reshape(D, N_TENSOR, local_kv, HD)
    weight_values = value_weight.reshape(D, N_TENSOR, local_kv, HD)

    def add_block(total, block):
        key_part = lax.dynamic_index_in_dim(key_blocks, block, 0, keepdims=False).astype(jnp.float32)
        value_part = lax.dynamic_index_in_dim(value_blocks, block, 0, keepdims=False).astype(jnp.float32)
        weight_k = lax.dynamic_index_in_dim(weight_keys, block, 1, keepdims=False).astype(jnp.float32)
        weight_v = lax.dynamic_index_in_dim(weight_values, block, 1, keepdims=False).astype(jnp.float32)
        partial_sum = jnp.einsum("gth,dgh->td", key_part, weight_k, precision=lax.Precision.HIGHEST)
        partial_sum = partial_sum + jnp.einsum("gth,dgh->td", value_part, weight_v, precision=lax.Precision.HIGHEST)
        rounded = lax.optimization_barrier(partial_sum.astype(jnp.bfloat16))
        return total + rounded.astype(jnp.float32), None

    total, _ = lax.scan(add_block, jnp.zeros((TOK, D), jnp.float32), jnp.arange(N_TENSOR, dtype=jnp.int32))
    input_grad = total.astype(jnp.bfloat16)
    key_flat = key_grad.transpose(1, 0, 2).reshape(TOK, KV * HD)
    value_flat = value_grad.transpose(1, 0, 2).reshape(TOK, KV * HD)
    projected = jnp.dot(hidden_in, in_basis, preferred_element_type=jnp.float32).astype(jnp.bfloat16)
    key_proj = jnp.dot(key_flat, key_basis, preferred_element_type=jnp.float32)
    value_proj = jnp.dot(value_flat, value_basis, preferred_element_type=jnp.float32)
    onehot = (doc_ids[:, None] == jnp.arange(DOCS, dtype=jnp.int32)[None, :]).astype(jnp.float32)
    weighted = (onehot[:, :, None] * projected.astype(jnp.float32)[:, None, :]).reshape(TOK, DOCS * RANK)
    key_docs = doc_outer(weighted, key_proj).reshape(DOCS, RANK, RANK)
    value_docs = doc_outer(weighted, value_proj).reshape(DOCS, RANK, RANK)
    return input_grad, key_docs, value_docs
```

```python
import functools
import math

import jax
import jax.numpy as jnp
from jax import lax
from jax.experimental import pallas as pl
from jax.experimental.pallas import tpu as pltpu
from jax.sharding import PartitionSpec as P

HD = 128
RANK = 64
DOCS = 8
QB = 128
CHIPS_Z, CHIPS_Y, CORES = 4, 2, 2
CHIPS = CHIPS_Z * CHIPS_Y
MIB = 1 << 20


def allowed_pairs(doc_ids):
    count = doc_ids.shape[0]
    position = jnp.arange(count, dtype=jnp.int32)
    same_doc = doc_ids[:, None] == doc_ids[None, :]
    return same_doc & (position[None, :] <= position[:, None])


def group_grads(query_heads, key_head, value_head, grad_heads, allowed):
    scale = HD ** (-0.5)

    def one_head(carry, operands):
        query, grad_out = operands
        scores = jnp.dot(query, key_head.T, preferred_element_type=jnp.float32) * scale
        scores = jnp.where(allowed, scores, -1e30)
        peak = jnp.max(scores, axis=1, keepdims=True)
        expo = jnp.exp(scores - peak)
        probs = expo / jnp.sum(expo, axis=1, keepdims=True)
        probs_low = probs.astype(jnp.bfloat16)
        value_step = lax.dot_general(
            probs_low, grad_out, (((0,), (0,)), ((), ())), preferred_element_type=jnp.float32
        )
        dprobs = jnp.dot(grad_out, value_head.T, preferred_element_type=jnp.float32)
        delta = jnp.sum(probs * dprobs, axis=1, keepdims=True)
        dscores = (probs * (dprobs - delta)).astype(jnp.bfloat16)
        key_step = (
            lax.dot_general(
                dscores, query, (((0,), (0,)), ((), ())), preferred_element_type=jnp.float32
            )
            * scale
        )
        return ((carry[0] + key_step, carry[1] + value_step), None)

    zeros = jnp.zeros((query_heads.shape[1], query_heads.shape[2]), jnp.float32)
    (key_sum, value_sum), _ = lax.scan(one_head, (zeros, zeros), (query_heads, grad_heads))
    return (key_sum.astype(jnp.bfloat16), value_sum.astype(jnp.bfloat16))


def doc_outer(weighted, grads):
    return lax.dot_general(
        weighted,
        grads,
        (((0,), (0,)), ((), ())),
        precision=lax.Precision.HIGHEST,
        preferred_element_type=jnp.float32,
    )


def spread_docs(doc_ids, doc_first, doc_count, projected):
    tok_count = doc_ids.shape[0]
    doc_range = doc_first + jnp.arange(doc_count, dtype=jnp.int32)
    onehot = (doc_ids[:, None] == doc_range[None, :]).astype(jnp.float32)
    return (onehot[:, :, None] * projected.astype(jnp.float32)[:, None, :]).reshape(
        tok_count, doc_count * RANK
    )


def general_body(
    hidden_in,
    queries,
    keys,
    values,
    out_grad,
    key_weight,
    value_weight,
    in_basis,
    key_basis,
    value_basis,
    doc_ids,
):
    tok_count = doc_ids.shape[0]
    tp_size = lax.axis_size("tensor")
    tp_index = lax.axis_index("tensor")
    local_kv = keys.shape[1] // HD
    local_q = queries.shape[1] // HD
    group = local_q // local_kv
    allowed = allowed_pairs(doc_ids)
    query_heads = queries.reshape(tok_count, local_kv, group, HD).transpose(1, 2, 0, 3)
    grad_heads = out_grad.reshape(tok_count, local_kv, group, HD).transpose(1, 2, 0, 3)
    key_heads = keys.reshape(tok_count, local_kv, HD).transpose(1, 0, 2)
    value_heads = values.reshape(tok_count, local_kv, HD).transpose(1, 0, 2)
    key_grad, value_grad = lax.map(
        lambda ops: group_grads(ops[0], ops[1], ops[2], ops[3], allowed),
        (query_heads, key_heads, value_heads, grad_heads),
    )
    key_flat = key_grad.transpose(1, 0, 2).reshape(tok_count, local_kv * HD)
    value_flat = value_grad.transpose(1, 0, 2).reshape(tok_count, local_kv * HD)
    summed = lax.dot_general(
        key_flat, key_weight, (((1,), (1,)), ((), ())), preferred_element_type=jnp.float32
    )
    input_grad = lax.psum_scatter(
        (
            summed
            + lax.dot_general(
                value_flat,
                value_weight,
                (((1,), (1,)), ((), ())),
                preferred_element_type=jnp.float32,
            )
        ).astype(jnp.bfloat16),
        "tensor",
        scatter_dimension=0,
        tiled=True,
    )
    projected = jnp.dot(
        lax.all_gather(hidden_in, "tensor", axis=0, tiled=True),
        in_basis,
        preferred_element_type=jnp.float32,
    ).astype(jnp.bfloat16)
    key_part_proj = jnp.dot(key_flat, key_basis, preferred_element_type=jnp.float32)
    value_part_proj = jnp.dot(value_flat, value_basis, preferred_element_type=jnp.float32)
    docs_local = DOCS // tp_size
    key_proj, value_proj = (
        lax.psum(key_part_proj.astype(jnp.bfloat16), "tensor").astype(jnp.float32),
        lax.psum(value_part_proj.astype(jnp.bfloat16), "tensor").astype(jnp.float32),
    )
    weighted = spread_docs(doc_ids, tp_index * docs_local, docs_local, projected)
    key_docs = doc_outer(weighted, key_proj).reshape(docs_local, RANK, RANK)
    value_docs = doc_outer(weighted, value_proj).reshape(docs_local, RANK, RANK)
    return (input_grad, key_docs, value_docs)


def chip_at(place):
    place %= CHIPS
    return (place, 0) if place < CHIPS_Z else (CHIPS - 1 - place, 1)


def place_of(z, y):
    return z if y == 0 else CHIPS - 1 - z


def device(z, y, core, x):
    return ((z * CHIPS_Y + y) * CORES + core) * 2 + x


def pairs(move):
    out = []
    for z in range(CHIPS_Z):
        for y in range(CHIPS_Y):
            for core in range(CORES):
                for x in range(2):
                    out.append((device(z, y, core, x), device(*move(z, y, core, x))))
    return out


def send_x(a):
    return lax.ppermute(a, ("dp", "tensor"), pairs(lambda z, y, c, x: (z, y, c, 1 - x)))


def send_core(a):
    return lax.ppermute(a, ("dp", "tensor"), pairs(lambda z, y, c, x: (z, y, 1 - c, x)))


def send_ring(a, step):
    def move(z, y, c, x):
        to = chip_at(place_of(z, y) + step)
        return (to[0], to[1], c, x)

    return lax.ppermute(a, ("dp", "tensor"), pairs(move))


def attention_kernel(scal, docq, dock, q_ref, do_ref, k_ref, v_ref, own_ref, send_ref, acck, accv):
    tok = q_ref.shape[0]
    heads = q_ref.shape[1] // HD
    scale = HD ** (-0.5)
    c2 = scale * math.log2(math.e)
    acck[...] = jnp.zeros_like(acck)
    accv[...] = jnp.zeros_like(accv)
    nt = (((1,), (1,)), ((), ()))
    nn = (((1,), (0,)), ((), ()))
    f32 = jnp.float32
    for i in range(tok // QB):
        lo = max(i - 2, 0) * QB
        wide = (i + 1) * QB - lo
        rows = slice(i * QB, (i + 1) * QB)
        keys = k_ref[lo : lo + wide, :]
        vals = v_ref[lo : lo + wide, :]
        kpos = lo + lax.broadcasted_iota(jnp.int32, (wide, QB), 0)
        qpos = i * QB + lax.broadcasted_iota(jnp.int32, (wide, QB), 1)
        ok = (dock[lo : lo + wide, :] == docq[:, rows]) & (kpos <= qpos)
        bias = jnp.where(ok, 0.0, -1e30).astype(f32)
        bias2 = jnp.concatenate([bias, bias], axis=1)
        for pair in range(heads // 2):
            cols = [slice((2 * pair + n) * HD, (2 * pair + n + 1) * HD) for n in range(2)]
            q = jnp.concatenate([q_ref[rows, c] for c in cols], axis=0)
            do = jnp.concatenate([do_ref[rows, c] for c in cols], axis=0)
            s = lax.dot_general(keys, q, nt, preferred_element_type=f32) + bias2
            dp = lax.dot_general(vals, do, nt, preferred_element_type=f32)
            peak = jnp.max(s, axis=0, keepdims=True)
            e = jnp.exp2((s - peak) * c2)
            inv = 1.0 / jnp.sum(e, axis=0, keepdims=True)
            p = e * inv
            delta = jnp.sum(p * dp, axis=0, keepdims=True)
            ds = (p * (dp - delta)).astype(jnp.bfloat16)
            accv[lo : lo + wide, :] += lax.dot_general(
                p.astype(jnp.bfloat16), do, nn, preferred_element_type=f32
            )
            acck[lo : lo + wide, :] += lax.dot_general(ds, q, nn, preferred_element_type=f32)
    half = tok // 2
    mine = pl.multiple_of(scal[0] * half, half)
    theirs = pl.multiple_of((1 - scal[0]) * half, half)
    for ref, start in ((own_ref, mine), (send_ref, theirs)):
        ref[:, :HD] = (acck[pl.ds(start, half), :] * scale).astype(jnp.bfloat16)
        ref[:, HD:] = accv[pl.ds(start, half), :].astype(jnp.bfloat16)


def attention(scal, docq, dock, queries, out_grad, keys, values, head):
    tok = queries.shape[0]
    group = queries.shape[1] // keys.shape[1]
    whole = lambda a: pl.BlockSpec(a.shape, lambda g, s: (0, 0))
    wide = pl.BlockSpec((tok, group * HD), lambda g, s: (0, head))
    narrow = pl.BlockSpec((tok, HD), lambda g, s: (0, head))
    out = jax.ShapeDtypeStruct((tok // 2, 2 * HD), jnp.bfloat16)
    out_spec = pl.BlockSpec(out.shape, lambda g, s: (0, 0))
    return pl.pallas_call(
        attention_kernel,
        out_shape=(out, out),
        grid_spec=pltpu.PrefetchScalarGridSpec(
            num_scalar_prefetch=1,
            grid=(1,),
            in_specs=[whole(docq), whole(dock), wide, wide, narrow, narrow],
            out_specs=(out_spec, out_spec),
            scratch_shapes=[pltpu.VMEM((tok, HD), jnp.float32)] * 2,
        ),
        compiler_params=pltpu.CompilerParams(vmem_limit_bytes=24 * MIB),
        cost_estimate=pl.CostEstimate(
            flops=8 * tok * 384 * HD * group, bytes_accessed=5 * MIB, transcendentals=tok * 384 * group
        ),
        name="attention_back",
    )(scal, docq, dock, queries, out_grad, keys, values)


def docs_kernel(scal, doc_own, doc_oth, proj_own, proj_oth, kb, vb, *refs):
    heads = kb.shape[1] // HD
    owns, sends = refs[:heads], refs[heads : 2 * heads]
    mine_ref, theirs_ref, total = refs[2 * heads :]
    f32 = jnp.float32
    nt = (((1,), (1,)), ((), ()))
    nn = (((1,), (0,)), ((), ()))
    for first, (doc, proj, parts) in enumerate(((doc_own, proj_own, owns), (doc_oth, proj_oth, sends))):
        gk = jnp.concatenate([r[:, :HD] for r in parts], axis=1)
        gv = jnp.concatenate([r[:, HD:] for r in parts], axis=1)
        pk = lax.dot_general(gk, kb[...], nt, preferred_element_type=f32)
        pv = lax.dot_general(gv, vb[...], nt, preferred_element_type=f32)
        both = jnp.concatenate([pk, pv], axis=1)
        high = both.astype(jnp.bfloat16)
        low = (both - high.astype(f32)).astype(jnp.bfloat16)
        p = proj[...].astype(f32)
        ids = doc[...]
        w = jnp.concatenate(
            [jnp.where(ids == d, p, 0.0) for d in range(DOCS)], axis=0
        ).astype(jnp.bfloat16)
        add = lax.dot_general(w, high, nn, preferred_element_type=f32)
        add += lax.dot_general(w, low, nn, preferred_element_type=f32)
        if first == 0:
            total[...] = add
        else:
            total[...] += add
    half = total.shape[0] // 2
    mine_ref[...] = total[pl.ds(pl.multiple_of(scal[0] * half, half), half), :]
    theirs_ref[...] = total[pl.ds(pl.multiple_of((1 - scal[0]) * half, half), half), :]


def doc_sums(scal, doc_own, doc_oth, proj_own, proj_oth, kb, vb, owns, sends):
    args = (doc_own, doc_oth, proj_own, proj_oth, kb, vb, *owns, *sends)
    rows = DOCS * RANK
    out = jax.ShapeDtypeStruct((rows // 2, 2 * RANK), jnp.float32)
    spec = lambda a: pl.BlockSpec(a.shape, lambda g, s: (0, 0))
    return pl.pallas_call(
        docs_kernel,
        out_shape=(out, out),
        grid_spec=pltpu.PrefetchScalarGridSpec(
            num_scalar_prefetch=1,
            grid=(1,),
            in_specs=[spec(a) for a in args],
            out_specs=(spec(out), spec(out)),
            scratch_shapes=[pltpu.VMEM((rows, 2 * RANK), jnp.float32)],
        ),
        compiler_params=pltpu.CompilerParams(vmem_limit_bytes=24 * MIB),
        cost_estimate=pl.CostEstimate(flops=10**9, bytes_accessed=3 * MIB, transcendentals=0),
        name="doc_sums",
    )(scal, *args)


def slabs_kernel(widths, heads, aliased, scal, *refs):
    owns, others = refs[:heads], refs[heads : 2 * heads]
    at = 2 * heads
    wk, wv = refs[at : at + 2]
    at += 2
    n = len(widths)
    parts = [refs[at + 4 * s : at + 4 * s + 4] for s in range(n)]
    at += 4 * n + aliased
    out = refs[at]
    g, w = refs[at + 1], refs[at + 2 : at + 2 + n]
    o = refs[at + 2 + n : at + 2 + 2 * n]
    sem_g, sem_w, sem_o = refs[at + 2 + 2 * n :]
    core = scal[0]
    k = heads * HD
    copies = []
    for h in range(heads):
        first = pl.multiple_of(2 * k + core * k + h * HD, HD)
        second = pl.multiple_of(2 * k + (1 - core) * k + h * HD, HD)
        for src, dst in (
            (owns[h].at[:, :HD], g.at[:, h * HD : (h + 1) * HD]),
            (owns[h].at[:, HD:], g.at[:, k + h * HD : k + (h + 1) * HD]),
            (others[h].at[:, :HD], g.at[:, pl.ds(first, HD)]),
            (others[h].at[:, HD:], g.at[:, pl.ds(second, HD)]),
        ):
            copies.append(pltpu.make_async_copy(src, dst, sem_g.at[len(copies)]))
    for copy in copies:
        copy.start()
    loads = []
    for s in range(n):
        start = pl.multiple_of(scal[1 + s], HD)
        rows = pl.ds(start, widths[s])
        h = widths[s] // 2
        these = [
            (wk.at[rows, :], w[s].at[:, :k]),
            (wv.at[rows, :], w[s].at[:, k : 2 * k]),
            (parts[s][0], w[s].at[:h, 2 * k : 3 * k]),
            (parts[s][1], w[s].at[h:, 2 * k : 3 * k]),
            (parts[s][2], w[s].at[:h, 3 * k :]),
            (parts[s][3], w[s].at[h:, 3 * k :]),
        ]
        these = [pltpu.make_async_copy(a, b, sem_w.at[s, i]) for i, (a, b) in enumerate(these)]
        for copy in these:
            copy.start()
        loads.append(these)
    for copy in copies:
        copy.wait()
    stores = []
    for s in range(n):
        for copy in loads[s]:
            copy.wait()
        col = 0
        while col < widths[s]:
            size = min(256, widths[s] - col)
            o[s][:, col : col + size] = lax.dot_general(
                g[...],
                w[s][col : col + size, :],
                (((1,), (1,)), ((), ())),
                preferred_element_type=jnp.float32,
            ).astype(jnp.bfloat16)
            col += size
        start = pl.multiple_of(scal[1 + s], HD)
        copy = pltpu.make_async_copy(o[s], out.at[:, pl.ds(start, widths[s])], sem_o.at[s])
        copy.start()
        stores.append(copy)
    for copy in stores:
        copy.wait()


def slabs(core, starts, widths, owns, others, wk, wv, parts, before=None):
    heads = len(owns)
    rows, depth = owns[0].shape[0], 4 * heads * HD
    n = len(widths)
    scal = jnp.stack([core, *starts]).astype(jnp.int32)
    args = [*owns, *others, wk, wv] + [a for four in parts for a in four]
    aliases = {}
    if before is not None:
        aliases = {len(args) + 1: 0}
        args.append(before)
    total = sum(widths)
    return pl.pallas_call(
        functools.partial(slabs_kernel, widths, heads, before is not None),
        out_shape=jax.ShapeDtypeStruct((rows, wk.shape[0]), jnp.bfloat16),
        grid_spec=pltpu.PrefetchScalarGridSpec(
            num_scalar_prefetch=1,
            grid=(1,),
            in_specs=[pl.BlockSpec(memory_space=pl.ANY)] * len(args),
            out_specs=pl.BlockSpec(memory_space=pl.ANY),
            scratch_shapes=[pltpu.VMEM((rows, depth), jnp.bfloat16)]
            + [pltpu.VMEM((width, depth), jnp.bfloat16) for width in widths]
            + [pltpu.VMEM((rows, width), jnp.bfloat16) for width in widths]
            + [
                pltpu.SemaphoreType.DMA((4 * heads,)),
                pltpu.SemaphoreType.DMA((n, 6)),
                pltpu.SemaphoreType.DMA((n,)),
            ],
        ),
        input_output_aliases=aliases,
        compiler_params=pltpu.CompilerParams(vmem_limit_bytes=32 * MIB),
        cost_estimate=pl.CostEstimate(
            flops=2 * rows * depth * total, bytes_accessed=2 * (depth + rows) * total, transcendentals=0
        ),
        name="slabs",
    )(scal, *args)


def plane_body(
    hidden_in,
    queries,
    keys,
    values,
    out_grad,
    key_weight,
    value_weight,
    in_basis,
    key_basis,
    value_basis,
    doc_ids,
):
    tok = doc_ids.shape[0]
    half = tok // 2
    x = lax.axis_index("tensor")
    dp = lax.axis_index("dp")
    z, y, core = dp // (CHIPS_Y * CORES), (dp // CORES) % CHIPS_Y, dp % CORES
    place = jnp.where(y == 0, z, CHIPS - 1 - z)
    rows = key_weight.shape[0]
    slab = rows * 7 // 8 // CHIPS // HD * HD
    rest = rows - slab * CHIPS
    piece = slab // 2

    def pick(start, size):
        return jnp.where(
            core == 0,
            lax.dynamic_slice_in_dim(key_weight, start, size, 0),
            lax.dynamic_slice_in_dim(value_weight, start, size, 0),
        )

    got = [[send_x(pick(place * slab + n * piece, piece)) for n in range(2)]]
    rest_got = [send_x(pick(slab * CHIPS + n * (rest // 2), rest // 2)) for n in range(2)]
    up, down = got[0], got[0]
    ups, downs = [up], [down]
    for _ in range(CHIPS // 2 - 1):
        up = [send_ring(a, 1) for a in up]
        down = [send_ring(a, -1) for a in down]
        ups.append(up)
        downs.append(down)
    far = [send_ring(up[0], 1), send_ring(down[1], -1)]
    both = lambda a: [*a, *[send_core(b) for b in a]]

    scal = x.astype(jnp.int32)[None]
    docq = doc_ids[None, :]
    dock = jnp.broadcast_to(doc_ids[:, None], (tok, QB))
    proj = lax.dot_general(
        in_basis, hidden_in, (((0,), (1,)), ((), ())), preferred_element_type=jnp.float32
    ).astype(jnp.bfloat16)
    proj_oth = send_x(proj)
    owns, sends, others = [], [], []
    for head in range(keys.shape[1] // HD):
        own, send = attention(scal, docq, dock, queries, out_grad, keys, values, head)
        owns.append(own)
        sends.append(send)
        others.append(send_x(send))
    doc_own = lax.dynamic_slice_in_dim(docq, x * half, half, 1)
    doc_oth = lax.dynamic_slice_in_dim(docq, (1 - x) * half, half, 1)
    mine, theirs = doc_sums(
        scal, doc_own, doc_oth, proj, proj_oth, key_basis.T, value_basis.T, owns, sends
    )
    docs = (mine + send_x(theirs)).reshape(DOCS // 2, RANK, 2 * RANK)

    at = lambda n: (place + n) % CHIPS * slab
    run = lambda starts, widths, parts, before=None: slabs(
        core, starts, widths, owns, others, key_weight, value_weight, parts, before
    )
    out = run(
        [at(0), jnp.int32(slab * CHIPS)], [slab, rest], [both(got[0]), both(rest_got)]
    )
    for n in range(1, CHIPS // 2):
        out = run([at(-n), at(n)], [slab, slab], [both(ups[n]), both(downs[n])], out)
    out = run([at(CHIPS // 2)], [slab], [both(far)], out)
    return out, docs[:, :, :RANK], docs[:, :, RANK:]


def solution(mesh):
    placed = (
        P(("dp", "tensor"), None),
        P("dp", "tensor"),
        P("dp", "tensor"),
        P("dp", "tensor"),
        P("dp", "tensor"),
        P(None, "tensor"),
        P(None, "tensor"),
        P(),
        P("tensor", None),
        P("tensor", None),
        P("dp"),
    )
    fits = dict(mesh.shape) == {"dp": CHIPS * CORES, "tensor": 2}
    return jax.shard_map(
        plane_body if fits else general_body,
        mesh=mesh,
        in_specs=placed,
        out_specs=(
            P(("dp", "tensor"), None),
            P(("dp", "tensor"), None, None),
            P(("dp", "tensor"), None, None),
        ),
        check_vma=False,
    )
```

```python
import functools
import math

import jax
import jax.numpy as jnp
from jax import lax
from jax.experimental import pallas as pl
from jax.experimental.pallas import tpu as pltpu
from jax.sharding import PartitionSpec as P

HD = 128
RANK = 64
DOCS = 8
QB = 128
CHIPS_Z, CHIPS_Y, CORES = 4, 2, 2
CHIPS = CHIPS_Z * CHIPS_Y
MIB = 1 << 20
VMEM = 60 * MIB
ATT_VMEM = 60 * MIB
COST = pl.CostEstimate(flops=6*10**9, bytes_accessed=10**5, transcendentals=0)
PAIR = 2
TILE = 256
X, CORE, SEND, REST, SLABS = 0, 1, 2, 4, 5


def allowed_pairs(doc_ids):
    count = doc_ids.shape[0]
    position = jnp.arange(count, dtype=jnp.int32)
    same_doc = doc_ids[:, None] == doc_ids[None, :]
    return same_doc & (position[None, :] <= position[:, None])


def group_grads(query_heads, key_head, value_head, grad_heads, allowed):
    scale = HD ** (-0.5)

    def one_head(carry, operands):
        query, grad_out = operands
        scores = jnp.dot(query, key_head.T, preferred_element_type=jnp.float32) * scale
        scores = jnp.where(allowed, scores, -1e30)
        peak = jnp.max(scores, axis=1, keepdims=True)
        expo = jnp.exp(scores - peak)
        probs = expo / jnp.sum(expo, axis=1, keepdims=True)
        probs_low = probs.astype(jnp.bfloat16)
        value_step = lax.dot_general(
            probs_low, grad_out, (((0,), (0,)), ((), ())), preferred_element_type=jnp.float32
        )
        dprobs = jnp.dot(grad_out, value_head.T, preferred_element_type=jnp.float32)
        delta = jnp.sum(probs * dprobs, axis=1, keepdims=True)
        dscores = (probs * (dprobs - delta)).astype(jnp.bfloat16)
        key_step = (
            lax.dot_general(
                dscores, query, (((0,), (0,)), ((), ())), preferred_element_type=jnp.float32
            )
            * scale
        )
        return ((carry[0] + key_step, carry[1] + value_step), None)

    zeros = jnp.zeros((query_heads.shape[1], query_heads.shape[2]), jnp.float32)
    (key_sum, value_sum), _ = lax.scan(one_head, (zeros, zeros), (query_heads, grad_heads))
    return (key_sum.astype(jnp.bfloat16), value_sum.astype(jnp.bfloat16))


def doc_outer(weighted, grads):
    return lax.dot_general(
        weighted,
        grads,
        (((0,), (0,)), ((), ())),
        precision=lax.Precision.HIGHEST,
        preferred_element_type=jnp.float32,
    )


def spread_docs(doc_ids, doc_first, doc_count, projected):
    tok_count = doc_ids.shape[0]
    doc_range = doc_first + jnp.arange(doc_count, dtype=jnp.int32)
    onehot = (doc_ids[:, None] == doc_range[None, :]).astype(jnp.float32)
    return (onehot[:, :, None] * projected.astype(jnp.float32)[:, None, :]).reshape(
        tok_count, doc_count * RANK
    )


def general_body(
    hidden_in,
    queries,
    keys,
    values,
    out_grad,
    key_weight,
    value_weight,
    in_basis,
    key_basis,
    value_basis,
    doc_ids,
):
    tok_count = doc_ids.shape[0]
    tp_size = lax.axis_size("tensor")
    tp_index = lax.axis_index("tensor")
    local_kv = keys.shape[1] // HD
    local_q = queries.shape[1] // HD
    group = local_q // local_kv
    allowed = allowed_pairs(doc_ids)
    query_heads = queries.reshape(tok_count, local_kv, group, HD).transpose(1, 2, 0, 3)
    grad_heads = out_grad.reshape(tok_count, local_kv, group, HD).transpose(1, 2, 0, 3)
    key_heads = keys.reshape(tok_count, local_kv, HD).transpose(1, 0, 2)
    value_heads = values.reshape(tok_count, local_kv, HD).transpose(1, 0, 2)
    key_grad, value_grad = lax.map(
        lambda ops: group_grads(ops[0], ops[1], ops[2], ops[3], allowed),
        (query_heads, key_heads, value_heads, grad_heads),
    )
    key_flat = key_grad.transpose(1, 0, 2).reshape(tok_count, local_kv * HD)
    value_flat = value_grad.transpose(1, 0, 2).reshape(tok_count, local_kv * HD)
    summed = lax.dot_general(
        key_flat, key_weight, (((1,), (1,)), ((), ())), preferred_element_type=jnp.float32
    )
    input_grad = lax.psum_scatter(
        (
            summed
            + lax.dot_general(
                value_flat,
                value_weight,
                (((1,), (1,)), ((), ())),
                preferred_element_type=jnp.float32,
            )
        ).astype(jnp.bfloat16),
        "tensor",
        scatter_dimension=0,
        tiled=True,
    )
    projected = jnp.dot(
        lax.all_gather(hidden_in, "tensor", axis=0, tiled=True),
        in_basis,
        preferred_element_type=jnp.float32,
    ).astype(jnp.bfloat16)
    key_part_proj = jnp.dot(key_flat, key_basis, preferred_element_type=jnp.float32)
    value_part_proj = jnp.dot(value_flat, value_basis, preferred_element_type=jnp.float32)
    docs_local = DOCS // tp_size
    key_proj, value_proj = (
        lax.psum(key_part_proj.astype(jnp.bfloat16), "tensor").astype(jnp.float32),
        lax.psum(value_part_proj.astype(jnp.bfloat16), "tensor").astype(jnp.float32),
    )
    weighted = spread_docs(doc_ids, tp_index * docs_local, docs_local, projected)
    key_docs = doc_outer(weighted, key_proj).reshape(docs_local, RANK, RANK)
    value_docs = doc_outer(weighted, value_proj).reshape(docs_local, RANK, RANK)
    return (input_grad, key_docs, value_docs)


def chip_at(place):
    place %= CHIPS
    return (place, 0) if place < CHIPS_Z else (CHIPS - 1 - place, 1)


def place_of(z, y):
    return z if y == 0 else CHIPS - 1 - z


def device(z, y, core, x):
    return ((z * CHIPS_Y + y) * CORES + core) * 2 + x


def pairs(move):
    out = []
    for z in range(CHIPS_Z):
        for y in range(CHIPS_Y):
            for core in range(CORES):
                for x in range(2):
                    out.append((device(z, y, core, x), device(*move(z, y, core, x))))
    return out


def send_x(a):
    return lax.ppermute(a, ("dp", "tensor"), pairs(lambda z, y, c, x: (z, y, c, 1 - x)))


def send_core(a):
    return lax.ppermute(a, ("dp", "tensor"), pairs(lambda z, y, c, x: (z, y, 1 - c, x)))


def send_ring(a, step):
    def move(z, y, c, x):
        to = chip_at(place_of(z, y) + step)
        return (to[0], to[1], c, x)

    return lax.ppermute(a, ("dp", "tensor"), pairs(move))


def attention_kernel(scal, start_ref, q_ref, do_ref, k_ref, v_ref, *refs):
    own_ref, send_ref, acck, accv = refs[-4:]
    tok = q_ref.shape[0]
    heads = q_ref.shape[1] // HD
    scale = HD ** (-0.5)
    c2 = scale * math.log2(math.e)
    acck[...] = jnp.zeros_like(acck)
    accv[...] = jnp.zeros_like(accv)
    nt = (((1,), (1,)), ((), ()))
    nn = (((1,), (0,)), ((), ()))
    f32 = jnp.float32
    wide = 3 * QB
    kpos = lax.broadcasted_iota(jnp.int32, (wide, QB), 0)
    qpos = lax.broadcasted_iota(jnp.int32, (wide, QB), 1)

    @pl.loop(0, tok // QB, unroll=4)
    def _(i):
        lo = jnp.maximum(i - 2, 0) * QB
        rows = pl.ds(pl.multiple_of(i * QB, QB), QB)
        window = pl.ds(pl.multiple_of(lo, QB), wide)
        keys = k_ref[window, :]
        vals = v_ref[window, :]
        ok = (kpos >= start_ref[:, rows] - lo) & (kpos - qpos <= i * QB - lo)
        bias = jnp.where(ok, 0.0, -1e30).astype(f32)
        bias = jnp.concatenate([bias] * heads, axis=1)
        cols = [slice(n * HD, (n + 1) * HD) for n in range(heads)]
        q = jnp.concatenate([q_ref[rows, c] for c in cols], axis=0)
        do = jnp.concatenate([do_ref[rows, c] for c in cols], axis=0)
        s = lax.dot_general(keys, q, nt, preferred_element_type=f32) + bias
        dp = lax.dot_general(vals, do, nt, preferred_element_type=f32)
        peak = jnp.max(s, axis=0, keepdims=True)
        e = jnp.exp2((s - peak) * c2)
        inv = 1.0 / jnp.sum(e, axis=0, keepdims=True)
        delta = jnp.sum(e * dp, axis=0, keepdims=True) * inv
        p = e * inv
        ds = (p * (dp - delta)).astype(jnp.bfloat16)
        accv[window, :] += lax.dot_general(
            p.astype(jnp.bfloat16), do, nn, preferred_element_type=f32
        )
        acck[window, :] += lax.dot_general(ds, q, nn, preferred_element_type=f32)

    half = tok // 2
    mine = pl.multiple_of(scal[X] * half, half)
    theirs = pl.multiple_of((1 - scal[X]) * half, half)
    for ref, start in ((own_ref, mine), (send_ref, theirs)):
        ref[:, :HD] = (acck[pl.ds(start, half), :] * scale).astype(jnp.bfloat16)
        ref[:, HD:] = accv[pl.ds(start, half), :].astype(jnp.bfloat16)


def attention(scal, start, queries, out_grad, keys, values, head, waits, before):
    tok = queries.shape[0]
    group = queries.shape[1] // keys.shape[1]
    wide = pl.BlockSpec((tok, group * HD), lambda g, s: (0, head))
    narrow = pl.BlockSpec((tok, HD), lambda g, s: (0, head))
    out = jax.ShapeDtypeStruct((tok // 2, 2 * PAIR * HD), jnp.bfloat16)
    out_spec = pl.BlockSpec((tok // 2, 2 * HD), lambda g, s: (0, head % PAIR))
    args = [start, queries, out_grad, keys, values, *waits, *before]
    return pl.pallas_call(
        attention_kernel,
        out_shape=(out, out),
        grid_spec=pltpu.PrefetchScalarGridSpec(
            num_scalar_prefetch=1,
            grid=(1,),
            in_specs=[pl.BlockSpec(start.shape, lambda g, s: (0, 0)), wide, wide, narrow, narrow]
            + [pl.BlockSpec(memory_space=pl.ANY)] * (len(args) - 5),
            out_specs=(out_spec, out_spec),
            scratch_shapes=[pltpu.VMEM((tok, HD), jnp.float32)] * 2,
        ),
        input_output_aliases={len(args) - 1 + n: n for n in range(len(before))},
        compiler_params=pltpu.CompilerParams(vmem_limit_bytes=ATT_VMEM),
        cost_estimate=COST,
        name="attention_back",
    )(scal, *args)


def docs_kernel(scal, doc_own, doc_oth, proj_own, proj_oth, kb, vb, *refs):
    heads = kb.shape[1] // HD
    owns, sends = refs[: heads // PAIR], refs[heads // PAIR : 2 * heads // PAIR]
    mine_ref, theirs_ref, total = refs[-3:]
    f32 = jnp.float32
    nt = (((1,), (1,)), ((), ()))
    nn = (((1,), (0,)), ((), ()))
    for first, (doc, proj, parts) in enumerate(((doc_own, proj_own, owns), (doc_oth, proj_oth, sends))):
        cut = lambda n: [r[:, a : a + HD] for r in parts for a in range(n * HD, r.shape[1], 2 * HD)]
        gk = jnp.concatenate(cut(0), axis=1)
        gv = jnp.concatenate(cut(1), axis=1)
        pk = lax.dot_general(gk, kb[...], nt, preferred_element_type=f32)
        pv = lax.dot_general(gv, vb[...], nt, preferred_element_type=f32)
        both = jnp.concatenate([pk, pv], axis=1)
        high = both.astype(jnp.bfloat16)
        low = (both - high.astype(f32)).astype(jnp.bfloat16)
        p = proj[...].astype(f32)
        ids = doc[...]
        w = jnp.concatenate(
            [jnp.where(ids == d, p, 0.0) for d in range(DOCS)], axis=0
        ).astype(jnp.bfloat16)
        add = lax.dot_general(w, high, nn, preferred_element_type=f32)
        add += lax.dot_general(w, low, nn, preferred_element_type=f32)
        if first == 0:
            total[...] = add
        else:
            total[...] += add
    half = total.shape[0] // 2
    mine_ref[...] = total[pl.ds(pl.multiple_of(scal[X] * half, half), half), :]
    theirs_ref[...] = total[pl.ds(pl.multiple_of((1 - scal[X]) * half, half), half), :]


def doc_sums(scal, doc_own, doc_oth, proj_own, proj_oth, kb, vb, owns, sends, waits):
    args = (doc_own, doc_oth, proj_own, proj_oth, kb, vb, *owns, *sends)
    rows = DOCS * RANK
    out = jax.ShapeDtypeStruct((rows // 2, 2 * RANK), jnp.float32)
    spec = lambda a: pl.BlockSpec(a.shape, lambda g, s: (0, 0))
    return pl.pallas_call(
        docs_kernel,
        out_shape=(out, out),
        grid_spec=pltpu.PrefetchScalarGridSpec(
            num_scalar_prefetch=1,
            grid=(1,),
            in_specs=[spec(a) for a in args] + [pl.BlockSpec(memory_space=pl.ANY)] * len(waits),
            out_specs=(spec(out), spec(out)),
            scratch_shapes=[pltpu.VMEM((rows, 2 * RANK), jnp.float32)],
        ),
        compiler_params=pltpu.CompilerParams(vmem_limit_bytes=VMEM),
        cost_estimate=COST,
        name="doc_sums",
    )(scal, *args, *waits)


def join_kernel(scal, *refs):
    out = refs[-1]
    n = out.shape[1] // HD // 4
    k = n * HD
    key, value = [], []
    for ref in refs[: 2 * n // PAIR]:
        for h in range(PAIR):
            key.append((ref, slice(2 * h * HD, (2 * h + 1) * HD)))
            value.append((ref, slice((2 * h + 1) * HD, (2 * h + 2) * HD)))
    for h in range(n):
        for q, side in enumerate((key, value)):
            ref, cols = side[h]
            out[:, q * k + h * HD : q * k + (h + 1) * HD] = ref[:, cols]
    for core in range(2):

        @pl.when(scal[CORE] == core)
        def _():
            for h in range(n):
                for q, side in enumerate((key, value)):
                    ref, cols = side[n + h]
                    at = 2 * k + (q ^ core) * k + h * HD
                    out[:, at : at + HD] = ref[:, cols]


def join(scal, owns, others, waits):
    args = (*owns, *others)
    rows = owns[0].shape[0]
    out = jax.ShapeDtypeStruct((rows, sum(a.shape[1] for a in args)), jnp.bfloat16)
    spec = lambda a: pl.BlockSpec(a.shape, lambda g, s: (0, 0))
    return pl.pallas_call(
        join_kernel,
        out_shape=out,
        grid_spec=pltpu.PrefetchScalarGridSpec(
            num_scalar_prefetch=1,
            grid=(1,),
            in_specs=[spec(a) for a in args] + [pl.BlockSpec(memory_space=pl.ANY)] * len(waits),
            out_specs=spec(out),
        ),
        compiler_params=pltpu.CompilerParams(vmem_limit_bytes=VMEM),
        cost_estimate=COST,
        name="join",
    )(scal, *args, *waits)


def slabs_kernel(widths, places, counts, extra, scal, g_hbm, wk, wv, *refs):
    n = len(widths)
    out, g, w, o, sem_g, sem_w, sem_o = refs[sum(counts) + extra :]
    k = wk.shape[1]
    total = sum(widths)
    begin = [sum(widths[:s]) for s in range(n)]
    load_g = pltpu.make_async_copy(g_hbm, g, sem_g)
    load_g.start()
    loads, stores = [], []
    for s in range(n):
        rows = pl.ds(pl.multiple_of(scal[places[s]], HD), widths[s])
        a, b = begin[s], begin[s] + widths[s]
        pieces = [(wk.at[rows, :], w.at[0, a:b]), (wv.at[rows, :], w.at[1, a:b])]
        these = refs[sum(counts[:s]) : sum(counts[: s + 1])]
        step = (b - a) // (counts[s] // 2)
        for q, ref in enumerate(these):
            to = a + q % (counts[s] // 2) * step
            pieces.append((ref, w.at[2 + q // (counts[s] // 2), to : to + step]))
        loads.append([pltpu.make_async_copy(c, d, sem_w.at[s, i]) for i, (c, d) in enumerate(pieces)])
        stores.append(pltpu.make_async_copy(o.at[:, a:b], out.at[:, rows], sem_o.at[s]))

    def begin_loads(s):
        for copy in loads[s]:
            copy.start()

    def end_loads(s):
        for copy in loads[s]:
            copy.wait()

    begin_loads(0)
    load_g.wait()
    end_loads(0)
    if n > 1:
        begin_loads(1)
    cuts = [b // TILE for b in begin]

    @pl.loop(0, total // TILE)
    def _(t):
        for s in range(1, n):

            @pl.when(t == cuts[s])
            def _():
                end_loads(s)
                if s + 1 < n:
                    begin_loads(s + 1)

        rows = pl.ds(pl.multiple_of(t * TILE, TILE), TILE)
        o[:, rows] = sum(
            lax.dot_general(
                g[:, q * k : (q + 1) * k],
                w[q, rows, :],
                (((1,), (1,)), ((), ())),
                preferred_element_type=jnp.float32,
            )
            for q in range(4)
        ).astype(jnp.bfloat16)
        for s in range(n - 1):

            @pl.when(t == (begin[s] + widths[s] - 1) // TILE)
            def _():
                stores[s].start()

    left = total % TILE
    if left:
        o[:, total - left :] = sum(
            lax.dot_general(
                g[:, q * k : (q + 1) * k],
                w[q, total - left :, :],
                (((1,), (1,)), ((), ())),
                preferred_element_type=jnp.float32,
            )
            for q in range(4)
        ).astype(jnp.bfloat16)
    stores[-1].start()
    for copy in stores:
        copy.wait()


def slabs(scal, places, g, wk, wv, parts, waits, before=None):
    rows, depth = g.shape
    n = len(parts)
    counts = [len(part) for part in parts]
    widths = [sum(a.shape[0] for a in part) // 2 for part in parts]
    args = [g, wk, wv] + [a for part in parts for a in part] + waits
    aliases = {}
    if before is not None:
        aliases = {len(args) + 1: 0}
        args.append(before)
    total = sum(widths)
    return pl.pallas_call(
        functools.partial(slabs_kernel, widths, places, counts, len(waits) + (before is not None)),
        out_shape=jax.ShapeDtypeStruct((rows, wk.shape[0]), jnp.bfloat16),
        grid_spec=pltpu.PrefetchScalarGridSpec(
            num_scalar_prefetch=1,
            grid=(1,),
            in_specs=[pl.BlockSpec(memory_space=pl.ANY)] * len(args),
            out_specs=pl.BlockSpec(memory_space=pl.ANY),
            scratch_shapes=[
                pltpu.VMEM((rows, depth), jnp.bfloat16),
                pltpu.VMEM((4, total, wk.shape[1]), jnp.bfloat16),
                pltpu.VMEM((rows, total), jnp.bfloat16),
                pltpu.SemaphoreType.DMA,
                pltpu.SemaphoreType.DMA((n, 6)),
                pltpu.SemaphoreType.DMA((n,)),
            ],
        ),
        input_output_aliases=aliases,
        compiler_params=pltpu.CompilerParams(vmem_limit_bytes=VMEM),
        cost_estimate=COST,
        name="slabs",
    )(scal, *args)


def pick_kernel(at, scal, wk, wv, *refs):
    out, sem = refs[-2:]
    size = out.shape[0]
    rows = pl.ds(pl.multiple_of(scal[at], 64), size)
    for core, ref in enumerate((wk, wv)):

        @pl.when(scal[CORE] == core)
        def _():
            copy = pltpu.make_async_copy(ref.at[rows, :], out, sem)
            copy.start()
            copy.wait()


def pick(scal, at, size, wk, wv, waits=()):
    spec = pl.BlockSpec(memory_space=pl.ANY)
    return pl.pallas_call(
        functools.partial(pick_kernel, at),
        out_shape=jax.ShapeDtypeStruct((size, wk.shape[1]), wk.dtype),
        grid_spec=pltpu.PrefetchScalarGridSpec(
            num_scalar_prefetch=1,
            grid=(1,),
            in_specs=[spec] * (2 + len(waits)),
            out_specs=pl.BlockSpec((size, wk.shape[1]), lambda g, s: (0, 0)),
            scratch_shapes=[pltpu.SemaphoreType.DMA],
        ),
        compiler_params=pltpu.CompilerParams(vmem_limit_bytes=VMEM),
        cost_estimate=COST,
        name="pick",
    )(scal, wk, wv, *waits)


def plane_body(
    hidden_in,
    queries,
    keys,
    values,
    out_grad,
    key_weight,
    value_weight,
    in_basis,
    key_basis,
    value_basis,
    doc_ids,
):
    tok = doc_ids.shape[0]
    half = tok // 2
    x = lax.axis_index("tensor")
    dp = lax.axis_index("dp")
    z, y, core = dp // (CHIPS_Y * CORES), (dp // CORES) % CHIPS_Y, dp % CORES
    place = jnp.where(y == 0, z, CHIPS - 1 - z)
    rows = key_weight.shape[0]
    slab = rows * 7 // 8 // CHIPS // HD * HD
    rest = rows - slab * CHIPS
    piece = slab // 2

    weights = (key_weight, value_weight)
    first = slab * CHIPS
    mine = place * slab
    starts = [(place + n) % CHIPS * slab for n in range(CHIPS)]
    scal = jnp.stack(
        [x, core, mine, mine + piece, first, *starts, first]
    ).astype(jnp.int32)
    sent = [pick(scal, SEND + n, piece, *weights) for n in range(2)]
    got = [send_x(a) for a in sent]
    both = lambda a: [*a, *[send_core(b) for b in a]]
    own_slab = both(got)
    up, down = got, got
    ups, downs = [up], [down]
    for _ in range(CHIPS // 2 - 1):
        up = [send_ring(a, 1) for a in up]
        down = [send_ring(a, -1) for a in down]
        ups.append(up)
        downs.append(down)
    far = [send_ring(up[0], 1), send_ring(down[1], -1)]
    stage = lambda n, half: [ups[n][half], downs[n][half]]

    docq = doc_ids[None, :]
    start = jnp.sum(doc_ids[None, :] < doc_ids[:, None], axis=1, dtype=jnp.int32)[None, :]
    proj = lax.dot_general(
        in_basis, hidden_in, (((0,), (1,)), ((), ())), preferred_element_type=jnp.float32
    ).astype(jnp.bfloat16)
    proj_oth = send_x(proj)
    heads = keys.shape[1] // HD
    waits = [sent, got[:1], [*got, *stage(1, 0)], stage(1, 1)]
    waits += [[]] * (heads - len(waits))
    owns, sends, others, last = [], [], [], []
    for head in range(heads):
        before = last if head % PAIR else []
        order = [] if head % PAIR else last[:1]
        last = list(
            attention(
                scal, start, queries, out_grad, keys, values, head, waits[head] + order, before
            )
        )
        if head % PAIR == PAIR - 1:
            owns.append(last[0])
            sends.append(last[1])
            others.append(send_x(last[1]))
    rest_got = [send_x(pick(scal, REST, rest, *weights, got))]
    doc_own = lax.dynamic_slice_in_dim(docq, x * half, half, 1)
    doc_oth = lax.dynamic_slice_in_dim(docq, (1 - x) * half, half, 1)
    mine, theirs = doc_sums(
        scal, doc_own, doc_oth, proj, proj_oth, key_basis.T, value_basis.T, owns, sends, stage(2, 0)
    )
    docs = (mine + send_x(theirs)).reshape(DOCS // 2, RANK, 2 * RANK)

    g = join(scal, owns, others, stage(2, 1))
    ring = {0: own_slab, CHIPS // 2: both(far), None: both(rest_got)}
    for n in range(1, CHIPS // 2):
        ring[CHIPS - n], ring[n] = both(ups[n]), both(downs[n])
    out = None
    plan = (((0, 7, 1), stage(3, 0)), ((6, 2, None), stage(3, 1)), ((5, 3), []), ((4,), []))
    for group, waits in plan:
        places = [SLABS + (CHIPS if n is None else n) for n in group]
        out = slabs(scal, places, g, *weights, [ring[n] for n in group], waits, out)
    return out, docs[:, :, :RANK], docs[:, :, RANK:]


def solution(mesh):
    placed = (
        P(("dp", "tensor"), None),
        P("dp", "tensor"),
        P("dp", "tensor"),
        P("dp", "tensor"),
        P("dp", "tensor"),
        P(None, "tensor"),
        P(None, "tensor"),
        P(),
        P("tensor", None),
        P("tensor", None),
        P("dp"),
    )
    fits = dict(mesh.shape) == {"dp": CHIPS * CORES, "tensor": 2}
    return jax.shard_map(
        plane_body if fits else general_body,
        mesh=mesh,
        in_specs=placed,
        out_specs=(
            P(("dp", "tensor"), None),
            P(("dp", "tensor"), None, None),
            P(("dp", "tensor"), None, None),
        ),
        check_vma=False,
    )
```

```python
import functools
import math

import jax
import jax.numpy as jnp
from jax import lax
from jax.experimental import pallas as pl
from jax.experimental.pallas import tpu as pltpu
from jax.sharding import PartitionSpec as P

HD = 128
RANK = 64
DOCS = 8
QB = 128
CHIPS_Z, CHIPS_Y, CORES = 4, 2, 2
CHIPS = CHIPS_Z * CHIPS_Y
MIB = 1 << 20
VMEM = 52 * MIB
ATT_VMEM = 60 * MIB
COST = pl.CostEstimate(flops=5 * 10**9, bytes_accessed=10**5, transcendentals=0)
PAIR = 2
TILE = 896
X, CORE, SEND, REST, SLABS = 0, 1, 2, 4, 5


def allowed_pairs(doc_ids):
    count = doc_ids.shape[0]
    position = jnp.arange(count, dtype=jnp.int32)
    same_doc = doc_ids[:, None] == doc_ids[None, :]
    return same_doc & (position[None, :] <= position[:, None])


def group_grads(query_heads, key_head, value_head, grad_heads, allowed):
    scale = HD ** (-0.5)

    def one_head(carry, operands):
        query, grad_out = operands
        scores = jnp.dot(query, key_head.T, preferred_element_type=jnp.float32) * scale
        scores = jnp.where(allowed, scores, -1e30)
        peak = jnp.max(scores, axis=1, keepdims=True)
        expo = jnp.exp(scores - peak)
        probs = expo / jnp.sum(expo, axis=1, keepdims=True)
        probs_low = probs.astype(jnp.bfloat16)
        value_step = lax.dot_general(
            probs_low, grad_out, (((0,), (0,)), ((), ())), preferred_element_type=jnp.float32
        )
        dprobs = jnp.dot(grad_out, value_head.T, preferred_element_type=jnp.float32)
        delta = jnp.sum(probs * dprobs, axis=1, keepdims=True)
        dscores = (probs * (dprobs - delta)).astype(jnp.bfloat16)
        key_step = (
            lax.dot_general(
                dscores, query, (((0,), (0,)), ((), ())), preferred_element_type=jnp.float32
            )
            * scale
        )
        return ((carry[0] + key_step, carry[1] + value_step), None)

    zeros = jnp.zeros((query_heads.shape[1], query_heads.shape[2]), jnp.float32)
    (key_sum, value_sum), _ = lax.scan(one_head, (zeros, zeros), (query_heads, grad_heads))
    return (key_sum.astype(jnp.bfloat16), value_sum.astype(jnp.bfloat16))


def doc_outer(weighted, grads):
    return lax.dot_general(
        weighted,
        grads,
        (((0,), (0,)), ((), ())),
        precision=lax.Precision.HIGHEST,
        preferred_element_type=jnp.float32,
    )


def spread_docs(doc_ids, doc_first, doc_count, projected):
    tok_count = doc_ids.shape[0]
    doc_range = doc_first + jnp.arange(doc_count, dtype=jnp.int32)
    onehot = (doc_ids[:, None] == doc_range[None, :]).astype(jnp.float32)
    return (onehot[:, :, None] * projected.astype(jnp.float32)[:, None, :]).reshape(
        tok_count, doc_count * RANK
    )


def general_body(
    hidden_in,
    queries,
    keys,
    values,
    out_grad,
    key_weight,
    value_weight,
    in_basis,
    key_basis,
    value_basis,
    doc_ids,
):
    tok_count = doc_ids.shape[0]
    tp_size = lax.axis_size("tensor")
    tp_index = lax.axis_index("tensor")
    local_kv = keys.shape[1] // HD
    local_q = queries.shape[1] // HD
    group = local_q // local_kv
    allowed = allowed_pairs(doc_ids)
    query_heads = queries.reshape(tok_count, local_kv, group, HD).transpose(1, 2, 0, 3)
    grad_heads = out_grad.reshape(tok_count, local_kv, group, HD).transpose(1, 2, 0, 3)
    key_heads = keys.reshape(tok_count, local_kv, HD).transpose(1, 0, 2)
    value_heads = values.reshape(tok_count, local_kv, HD).transpose(1, 0, 2)
    key_grad, value_grad = lax.map(
        lambda ops: group_grads(ops[0], ops[1], ops[2], ops[3], allowed),
        (query_heads, key_heads, value_heads, grad_heads),
    )
    key_flat = key_grad.transpose(1, 0, 2).reshape(tok_count, local_kv * HD)
    value_flat = value_grad.transpose(1, 0, 2).reshape(tok_count, local_kv * HD)
    summed = lax.dot_general(
        key_flat, key_weight, (((1,), (1,)), ((), ())), preferred_element_type=jnp.float32
    )
    input_grad = lax.psum_scatter(
        (
            summed
            + lax.dot_general(
                value_flat,
                value_weight,
                (((1,), (1,)), ((), ())),
                preferred_element_type=jnp.float32,
            )
        ).astype(jnp.bfloat16),
        "tensor",
        scatter_dimension=0,
        tiled=True,
    )
    projected = jnp.dot(
        lax.all_gather(hidden_in, "tensor", axis=0, tiled=True),
        in_basis,
        preferred_element_type=jnp.float32,
    ).astype(jnp.bfloat16)
    key_part_proj = jnp.dot(key_flat, key_basis, preferred_element_type=jnp.float32)
    value_part_proj = jnp.dot(value_flat, value_basis, preferred_element_type=jnp.float32)
    docs_local = DOCS // tp_size
    key_proj, value_proj = (
        lax.psum(key_part_proj.astype(jnp.bfloat16), "tensor").astype(jnp.float32),
        lax.psum(value_part_proj.astype(jnp.bfloat16), "tensor").astype(jnp.float32),
    )
    weighted = spread_docs(doc_ids, tp_index * docs_local, docs_local, projected)
    key_docs = doc_outer(weighted, key_proj).reshape(docs_local, RANK, RANK)
    value_docs = doc_outer(weighted, value_proj).reshape(docs_local, RANK, RANK)
    return (input_grad, key_docs, value_docs)


def chip_at(place):
    place %= CHIPS
    return (place, 0) if place < CHIPS_Z else (CHIPS - 1 - place, 1)


def place_of(z, y):
    return z if y == 0 else CHIPS - 1 - z


def device(z, y, core, x):
    return ((z * CHIPS_Y + y) * CORES + core) * 2 + x


def pairs(move):
    out = []
    for z in range(CHIPS_Z):
        for y in range(CHIPS_Y):
            for core in range(CORES):
                for x in range(2):
                    out.append((device(z, y, core, x), device(*move(z, y, core, x))))
    return out


def send_x(a):
    return lax.ppermute(a, ("dp", "tensor"), pairs(lambda z, y, c, x: (z, y, c, 1 - x)))


def send_core(a):
    return lax.ppermute(a, ("dp", "tensor"), pairs(lambda z, y, c, x: (z, y, 1 - c, x)))


def send_ring(a, step):
    def move(z, y, c, x):
        to = chip_at(place_of(z, y) + step)
        return (to[0], to[1], c, x)

    return lax.ppermute(a, ("dp", "tensor"), pairs(move))


def attention_kernel(scal, start_ref, q_ref, do_ref, k_ref, v_ref, *refs):
    own_ref, send_ref, acck, accv = refs[-4:]
    tok = q_ref.shape[0]
    heads = q_ref.shape[1] // HD
    scale = HD ** (-0.5)
    c2 = scale * math.log2(math.e)
    acck[...] = jnp.zeros_like(acck)
    accv[...] = jnp.zeros_like(accv)
    nt = (((1,), (1,)), ((), ()))
    nn = (((1,), (0,)), ((), ()))
    f32 = jnp.float32
    wide = 3 * QB
    kpos = lax.broadcasted_iota(jnp.int32, (wide, QB), 0)
    qpos = lax.broadcasted_iota(jnp.int32, (wide, QB), 1)

    @pl.loop(0, tok // QB, unroll=4)
    def _(i):
        lo = jnp.maximum(i - 2, 0) * QB
        rows = pl.ds(pl.multiple_of(i * QB, QB), QB)
        window = pl.ds(pl.multiple_of(lo, QB), wide)
        keys = k_ref[window, :]
        vals = v_ref[window, :]
        ok = (kpos >= start_ref[:, rows] - lo) & (kpos - qpos <= i * QB - lo)
        bias = jnp.where(ok, 0.0, -1e30).astype(f32)
        bias = jnp.concatenate([bias] * heads, axis=1)
        cols = [slice(n * HD, (n + 1) * HD) for n in range(heads)]
        q = jnp.concatenate([q_ref[rows, c] for c in cols], axis=0)
        do = jnp.concatenate([do_ref[rows, c] for c in cols], axis=0)
        s = lax.dot_general(keys, q, nt, preferred_element_type=f32) + bias
        dp = lax.dot_general(vals, do, nt, preferred_element_type=f32)
        peak = jnp.max(s, axis=0, keepdims=True)
        e = jnp.exp2((s - peak) * c2)
        inv = 1.0 / jnp.sum(e, axis=0, keepdims=True)
        delta = jnp.sum(e * dp, axis=0, keepdims=True) * inv
        p = e * inv
        ds = (p * (dp - delta)).astype(jnp.bfloat16)
        accv[window, :] += lax.dot_general(
            p.astype(jnp.bfloat16), do, nn, preferred_element_type=f32
        )
        acck[window, :] += lax.dot_general(ds, q, nn, preferred_element_type=f32)

    half = tok // 2
    mine = pl.multiple_of(scal[X] * half, half)
    theirs = pl.multiple_of((1 - scal[X]) * half, half)
    for ref, start in ((own_ref, mine), (send_ref, theirs)):
        ref[:, :HD] = (acck[pl.ds(start, half), :] * scale).astype(jnp.bfloat16)
        ref[:, HD:] = accv[pl.ds(start, half), :].astype(jnp.bfloat16)


def attention(scal, start, queries, out_grad, keys, values, head, waits, before):
    tok = queries.shape[0]
    group = queries.shape[1] // keys.shape[1]
    wide = pl.BlockSpec((tok, group * HD), lambda g, s: (0, head))
    narrow = pl.BlockSpec((tok, HD), lambda g, s: (0, head))
    out = jax.ShapeDtypeStruct((tok // 2, 2 * PAIR * HD), jnp.bfloat16)
    out_spec = pl.BlockSpec((tok // 2, 2 * HD), lambda g, s: (0, head % PAIR))
    args = [start, queries, out_grad, keys, values, *waits, *before]
    return pl.pallas_call(
        attention_kernel,
        out_shape=(out, out),
        grid_spec=pltpu.PrefetchScalarGridSpec(
            num_scalar_prefetch=1,
            grid=(1,),
            in_specs=[pl.BlockSpec(start.shape, lambda g, s: (0, 0)), wide, wide, narrow, narrow]
            + [pl.BlockSpec(memory_space=pl.ANY)] * (len(args) - 5),
            out_specs=(out_spec, out_spec),
            scratch_shapes=[pltpu.VMEM((tok, HD), jnp.float32)] * 2,
        ),
        input_output_aliases={len(args) - 1 + n: n for n in range(len(before))},
        compiler_params=pltpu.CompilerParams(vmem_limit_bytes=ATT_VMEM),
        cost_estimate=COST,
        name="attention_back",
    )(scal, *args)


def docs_kernel(scal, doc_own, doc_oth, proj_own, proj_oth, kb, vb, *refs):
    heads = kb.shape[1] // HD
    owns, sends = refs[: heads // PAIR], refs[heads // PAIR : 2 * heads // PAIR]
    mine_ref, theirs_ref, total = refs[-3:]
    f32 = jnp.float32
    nt = (((1,), (1,)), ((), ()))
    nn = (((1,), (0,)), ((), ()))
    for first, (doc, proj, parts) in enumerate(((doc_own, proj_own, owns), (doc_oth, proj_oth, sends))):
        cut = lambda n: [r[:, a : a + HD] for r in parts for a in range(n * HD, r.shape[1], 2 * HD)]
        gk = jnp.concatenate(cut(0), axis=1)
        gv = jnp.concatenate(cut(1), axis=1)
        pk = lax.dot_general(gk, kb[...], nt, preferred_element_type=f32)
        pv = lax.dot_general(gv, vb[...], nt, preferred_element_type=f32)
        both = jnp.concatenate([pk, pv], axis=1)
        high = both.astype(jnp.bfloat16)
        low = (both - high.astype(f32)).astype(jnp.bfloat16)
        p = proj[...].astype(f32)
        ids = doc[...]
        w = jnp.concatenate(
            [jnp.where(ids == d, p, 0.0) for d in range(DOCS)], axis=0
        ).astype(jnp.bfloat16)
        add = lax.dot_general(w, high, nn, preferred_element_type=f32)
        add += lax.dot_general(w, low, nn, preferred_element_type=f32)
        if first == 0:
            total[...] = add
        else:
            total[...] += add
    half = total.shape[0] // 2
    mine_ref[...] = total[pl.ds(pl.multiple_of(scal[X] * half, half), half), :]
    theirs_ref[...] = total[pl.ds(pl.multiple_of((1 - scal[X]) * half, half), half), :]


def doc_sums(scal, doc_own, doc_oth, proj_own, proj_oth, kb, vb, owns, sends, waits):
    args = (doc_own, doc_oth, proj_own, proj_oth, kb, vb, *owns, *sends)
    rows = DOCS * RANK
    out = jax.ShapeDtypeStruct((rows // 2, 2 * RANK), jnp.float32)
    spec = lambda a: pl.BlockSpec(a.shape, lambda g, s: (0, 0))
    return pl.pallas_call(
        docs_kernel,
        out_shape=(out, out),
        grid_spec=pltpu.PrefetchScalarGridSpec(
            num_scalar_prefetch=1,
            grid=(1,),
            in_specs=[spec(a) for a in args] + [pl.BlockSpec(memory_space=pl.ANY)] * len(waits),
            out_specs=(spec(out), spec(out)),
            scratch_shapes=[pltpu.VMEM((rows, 2 * RANK), jnp.float32)],
        ),
        compiler_params=pltpu.CompilerParams(vmem_limit_bytes=VMEM),
        cost_estimate=COST,
        name="doc_sums",
    )(scal, *args, *waits)


def join_kernel(swap, scal, *refs):
    out = refs[-1]
    n = out.shape[1] // HD // 2
    k = n * HD
    for core in range(2 if swap else 1):

        @pl.when(scal[CORE] == core if swap else scal[CORE] >= 0)
        def _():
            for h in range(n):
                ref = refs[h // PAIR]
                for q in range(2):
                    at = (q ^ core) * k + h * HD
                    cols = slice((2 * (h % PAIR) + q) * HD, (2 * (h % PAIR) + q + 1) * HD)
                    out[:, at : at + HD] = ref[:, cols]


def join(scal, args, swap, waits):
    rows = args[0].shape[0]
    out = jax.ShapeDtypeStruct((rows, sum(a.shape[1] for a in args)), jnp.bfloat16)
    spec = lambda a: pl.BlockSpec(a.shape, lambda g, s: (0, 0))
    return pl.pallas_call(
        functools.partial(join_kernel, swap),
        out_shape=out,
        grid_spec=pltpu.PrefetchScalarGridSpec(
            num_scalar_prefetch=1,
            grid=(1,),
            in_specs=[spec(a) for a in args] + [pl.BlockSpec(memory_space=pl.ANY)] * len(waits),
            out_specs=spec(out),
        ),
        compiler_params=pltpu.CompilerParams(vmem_limit_bytes=VMEM),
        cost_estimate=COST,
        name="join",
    )(scal, *args, *waits)


def slabs_kernel(widths, places, counts, extra, scal, g_own, g_oth, wk, wv, *refs):
    n = len(widths)
    out, g, w, o, sem_g, sem_w, sem_o = refs[sum(counts) + extra :]
    k = wk.shape[1]
    total = sum(widths)
    begin = [sum(widths[:s]) for s in range(n)]
    load_g = [
        pltpu.make_async_copy(g_own, g.at[0], sem_g.at[0]),
        pltpu.make_async_copy(g_oth, g.at[1], sem_g.at[1]),
    ]
    for copy in load_g:
        copy.start()
    loads, stores = [], []
    for s in range(n):
        rows = pl.ds(pl.multiple_of(scal[places[s]], HD), widths[s])
        a, b = begin[s], begin[s] + widths[s]
        pieces = [(wk.at[rows, :], w.at[0, a:b]), (wv.at[rows, :], w.at[1, a:b])]
        these = refs[sum(counts[:s]) : sum(counts[: s + 1])]
        step = (b - a) // (counts[s] // 2)
        for q, ref in enumerate(these):
            to = a + q % (counts[s] // 2) * step
            pieces.append((ref, w.at[2 + q // (counts[s] // 2), to : to + step]))
        loads.append([pltpu.make_async_copy(c, d, sem_w.at[s, i]) for i, (c, d) in enumerate(pieces)])
        stores.append(pltpu.make_async_copy(o.at[:, a:b], out.at[:, rows], sem_o.at[s]))

    def begin_loads(s):
        for copy in loads[s]:
            copy.start()

    def end_loads(s):
        for copy in loads[s]:
            copy.wait()

    begin_loads(0)
    for copy in load_g:
        copy.wait()
    end_loads(0)
    if n > 1:
        begin_loads(1)
    cuts = [b // TILE for b in begin]

    @pl.loop(0, total // TILE)
    def _(t):
        for s in range(1, n):

            @pl.when(t == cuts[s])
            def _():
                end_loads(s)
                if s + 1 < n:
                    begin_loads(s + 1)

        rows = pl.ds(pl.multiple_of(t * TILE, TILE), TILE)
        o[:, rows] = sum(
            lax.dot_general(
                g[q // 2, :, q % 2 * k : (q % 2 + 1) * k],
                w[q, rows, :],
                (((1,), (1,)), ((), ())),
                preferred_element_type=jnp.float32,
            )
            for q in range(4)
        ).astype(jnp.bfloat16)
        for s in range(n - 1):

            @pl.when(t == (begin[s] + widths[s] - 1) // TILE)
            def _():
                stores[s].start()

    left = total % TILE
    if left:
        o[:, total - left :] = sum(
            lax.dot_general(
                g[q // 2, :, q % 2 * k : (q % 2 + 1) * k],
                w[q, total - left :, :],
                (((1,), (1,)), ((), ())),
                preferred_element_type=jnp.float32,
            )
            for q in range(4)
        ).astype(jnp.bfloat16)
    stores[-1].start()
    for copy in stores:
        copy.wait()


def slabs(scal, places, g, wk, wv, parts, waits, before=None):
    rows, depth = g[0].shape
    n = len(parts)
    counts = [len(part) for part in parts]
    widths = [sum(a.shape[0] for a in part) // 2 for part in parts]
    args = [*g, wk, wv] + [a for part in parts for a in part] + waits
    aliases = {}
    if before is not None:
        aliases = {len(args) + 1: 0}
        args.append(before)
    total = sum(widths)
    return pl.pallas_call(
        functools.partial(slabs_kernel, widths, places, counts, len(waits) + (before is not None)),
        out_shape=jax.ShapeDtypeStruct((rows, wk.shape[0]), jnp.bfloat16),
        grid_spec=pltpu.PrefetchScalarGridSpec(
            num_scalar_prefetch=1,
            grid=(1,),
            in_specs=[pl.BlockSpec(memory_space=pl.ANY)] * len(args),
            out_specs=pl.BlockSpec(memory_space=pl.ANY),
            scratch_shapes=[
                pltpu.VMEM((2, rows, depth), jnp.bfloat16),
                pltpu.VMEM((4, total, wk.shape[1]), jnp.bfloat16),
                pltpu.VMEM((rows, total), jnp.bfloat16),
                pltpu.SemaphoreType.DMA((2,)),
                pltpu.SemaphoreType.DMA((n, 6)),
                pltpu.SemaphoreType.DMA((n,)),
            ],
        ),
        input_output_aliases=aliases,
        compiler_params=pltpu.CompilerParams(vmem_limit_bytes=VMEM),
        cost_estimate=COST,
        name="slabs",
    )(scal, *args)


def pick_kernel(at, scal, wk, wv, *refs):
    out, sem = refs[-2:]
    size = out.shape[0]
    rows = pl.ds(pl.multiple_of(scal[at], 64), size)
    for core, ref in enumerate((wk, wv)):

        @pl.when(scal[CORE] == core)
        def _():
            copy = pltpu.make_async_copy(ref.at[rows, :], out, sem)
            copy.start()
            copy.wait()


def pick(scal, at, size, wk, wv, waits=()):
    spec = pl.BlockSpec(memory_space=pl.ANY)
    return pl.pallas_call(
        functools.partial(pick_kernel, at),
        out_shape=jax.ShapeDtypeStruct((size, wk.shape[1]), wk.dtype),
        grid_spec=pltpu.PrefetchScalarGridSpec(
            num_scalar_prefetch=1,
            grid=(1,),
            in_specs=[spec] * (2 + len(waits)),
            out_specs=pl.BlockSpec((size, wk.shape[1]), lambda g, s: (0, 0)),
            scratch_shapes=[pltpu.SemaphoreType.DMA],
        ),
        compiler_params=pltpu.CompilerParams(vmem_limit_bytes=VMEM),
        cost_estimate=COST,
        name="pick",
    )(scal, wk, wv, *waits)


def plane_body(
    hidden_in,
    queries,
    keys,
    values,
    out_grad,
    key_weight,
    value_weight,
    in_basis,
    key_basis,
    value_basis,
    doc_ids,
):
    tok = doc_ids.shape[0]
    half = tok // 2
    x = lax.axis_index("tensor")
    dp = lax.axis_index("dp")
    z, y, core = dp // (CHIPS_Y * CORES), (dp // CORES) % CHIPS_Y, dp % CORES
    place = jnp.where(y == 0, z, CHIPS - 1 - z)
    rows = key_weight.shape[0]
    slab = rows * 7 // 8 // CHIPS // HD * HD
    rest = rows - slab * CHIPS
    piece = slab // 2

    weights = (key_weight, value_weight)
    first = slab * CHIPS
    mine = place * slab
    starts = [(place + n) % CHIPS * slab for n in range(CHIPS)]
    scal = jnp.stack(
        [x, core, mine, mine + piece, first, *starts, first]
    ).astype(jnp.int32)
    sent = [pick(scal, SEND + n, piece, *weights) for n in range(2)]
    got = [send_x(a) for a in sent]
    both = lambda a: [*a, *[send_core(b) for b in a]]
    own_slab = both(got)
    up, down = got, got
    ups, downs = [up], [down]
    for _ in range(CHIPS // 2 - 1):
        up = [send_ring(a, 1) for a in up]
        down = [send_ring(a, -1) for a in down]
        ups.append(up)
        downs.append(down)
    far = [send_ring(up[0], 1), send_ring(down[1], -1)]
    stage = lambda n, half: [ups[n][half], downs[n][half]]

    docq = doc_ids[None, :]
    start = jnp.sum(doc_ids[None, :] < doc_ids[:, None], axis=1, dtype=jnp.int32)[None, :]
    proj = lax.dot_general(
        in_basis, hidden_in, (((0,), (1,)), ((), ())), preferred_element_type=jnp.float32
    ).astype(jnp.bfloat16)
    proj_oth = send_x(proj)
    heads = keys.shape[1] // HD
    rest_got = [send_x(pick(scal, REST, rest, *weights, got))]
    waits = [sent, got, stage(1, 0), stage(1, 1)]
    waits += [[]] * (heads - len(waits))
    owns, sends, others, last = [], [], [], []
    for head in range(heads):
        before = last if head % PAIR else []
        order = [] if head % PAIR else last[:1]
        last = list(
            attention(
                scal, start, queries, out_grad, keys, values, head, waits[head] + order, before
            )
        )
        if head % PAIR == PAIR - 1:
            owns.append(last[0])
            sends.append(last[1])
            others.append(send_x(last[1]))
    doc_own = lax.dynamic_slice_in_dim(docq, x * half, half, 1)
    doc_oth = lax.dynamic_slice_in_dim(docq, (1 - x) * half, half, 1)
    mine, theirs = doc_sums(
        scal, doc_own, doc_oth, proj, proj_oth, key_basis.T, value_basis.T, owns, sends, [*stage(2, 0), *rest_got]
    )
    docs = (mine + send_x(theirs)).reshape(DOCS // 2, RANK, 2 * RANK)

    g = [join(scal, owns, False, [*stage(2, 0), *stage(2, 1)]), join(scal, others, True, [])]
    ring = {0: own_slab, CHIPS // 2: both(far), None: both(rest_got)}
    for n in range(1, CHIPS // 2):
        ring[CHIPS - n], ring[n] = both(ups[n]), both(downs[n])
    out = None
    plan = (((0, 7, 1), []), ((6, 2), stage(3, 0)), ((5, 3, None), []), ((4,), []))
    for group, waits in plan:
        places = [SLABS + (CHIPS if n is None else n) for n in group]
        out = slabs(scal, places, g, *weights, [ring[n] for n in group], waits, out)
    return out, docs[:, :, :RANK], docs[:, :, RANK:]


def solution(mesh):
    placed = (
        P(("dp", "tensor"), None),
        P("dp", "tensor"),
        P("dp", "tensor"),
        P("dp", "tensor"),
        P("dp", "tensor"),
        P(None, "tensor"),
        P(None, "tensor"),
        P(),
        P("tensor", None),
        P("tensor", None),
        P("dp"),
    )
    fits = dict(mesh.shape) == {"dp": CHIPS * CORES, "tensor": 2}
    return jax.shard_map(
        plane_body if fits else general_body,
        mesh=mesh,
        in_specs=placed,
        out_specs=(
            P(("dp", "tensor"), None),
            P(("dp", "tensor"), None, None),
            P(("dp", "tensor"), None, None),
        ),
        check_vma=False,
    )
```

```python
import functools
import math

import jax
import jax.numpy as jnp
from jax import lax
from jax.experimental import pallas as pl
from jax.experimental.pallas import tpu as pltpu
from jax.sharding import PartitionSpec as P

HD = 128
RANK = 64
DOCS = 8
QB = 128
CHIPS_Z, CHIPS_Y, CORES = 4, 2, 2
CHIPS = CHIPS_Z * CHIPS_Y
MIB = 1 << 20
VMEM = 52 * MIB
ATT_VMEM = 52 * MIB
COST = pl.CostEstimate(flops=5 * 10**9, bytes_accessed=10**5, transcendentals=0)
PAIR = 2
TILE = 896
X, CORE, SEND, REST, SLABS = 0, 1, 2, 4, 5


def allowed_pairs(doc_ids):
    count = doc_ids.shape[0]
    position = jnp.arange(count, dtype=jnp.int32)
    same_doc = doc_ids[:, None] == doc_ids[None, :]
    return same_doc & (position[None, :] <= position[:, None])


def group_grads(query_heads, key_head, value_head, grad_heads, allowed):
    scale = HD ** (-0.5)

    def one_head(carry, operands):
        query, grad_out = operands
        scores = jnp.dot(query, key_head.T, preferred_element_type=jnp.float32) * scale
        scores = jnp.where(allowed, scores, -1e30)
        peak = jnp.max(scores, axis=1, keepdims=True)
        expo = jnp.exp(scores - peak)
        probs = expo / jnp.sum(expo, axis=1, keepdims=True)
        probs_low = probs.astype(jnp.bfloat16)
        value_step = lax.dot_general(
            probs_low, grad_out, (((0,), (0,)), ((), ())), preferred_element_type=jnp.float32
        )
        dprobs = jnp.dot(grad_out, value_head.T, preferred_element_type=jnp.float32)
        delta = jnp.sum(probs * dprobs, axis=1, keepdims=True)
        dscores = (probs * (dprobs - delta)).astype(jnp.bfloat16)
        key_step = (
            lax.dot_general(
                dscores, query, (((0,), (0,)), ((), ())), preferred_element_type=jnp.float32
            )
            * scale
        )
        return ((carry[0] + key_step, carry[1] + value_step), None)

    zeros = jnp.zeros((query_heads.shape[1], query_heads.shape[2]), jnp.float32)
    (key_sum, value_sum), _ = lax.scan(one_head, (zeros, zeros), (query_heads, grad_heads))
    return (key_sum.astype(jnp.bfloat16), value_sum.astype(jnp.bfloat16))


def doc_outer(weighted, grads):
    return lax.dot_general(
        weighted,
        grads,
        (((0,), (0,)), ((), ())),
        precision=lax.Precision.HIGHEST,
        preferred_element_type=jnp.float32,
    )


def spread_docs(doc_ids, doc_first, doc_count, projected):
    tok_count = doc_ids.shape[0]
    doc_range = doc_first + jnp.arange(doc_count, dtype=jnp.int32)
    onehot = (doc_ids[:, None] == doc_range[None, :]).astype(jnp.float32)
    return (onehot[:, :, None] * projected.astype(jnp.float32)[:, None, :]).reshape(
        tok_count, doc_count * RANK
    )


def general_body(
    hidden_in,
    queries,
    keys,
    values,
    out_grad,
    key_weight,
    value_weight,
    in_basis,
    key_basis,
    value_basis,
    doc_ids,
):
    tok_count = doc_ids.shape[0]
    tp_size = lax.axis_size("tensor")
    tp_index = lax.axis_index("tensor")
    local_kv = keys.shape[1] // HD
    local_q = queries.shape[1] // HD
    group = local_q // local_kv
    allowed = allowed_pairs(doc_ids)
    query_heads = queries.reshape(tok_count, local_kv, group, HD).transpose(1, 2, 0, 3)
    grad_heads = out_grad.reshape(tok_count, local_kv, group, HD).transpose(1, 2, 0, 3)
    key_heads = keys.reshape(tok_count, local_kv, HD).transpose(1, 0, 2)
    value_heads = values.reshape(tok_count, local_kv, HD).transpose(1, 0, 2)
    key_grad, value_grad = lax.map(
        lambda ops: group_grads(ops[0], ops[1], ops[2], ops[3], allowed),
        (query_heads, key_heads, value_heads, grad_heads),
    )
    key_flat = key_grad.transpose(1, 0, 2).reshape(tok_count, local_kv * HD)
    value_flat = value_grad.transpose(1, 0, 2).reshape(tok_count, local_kv * HD)
    summed = lax.dot_general(
        key_flat, key_weight, (((1,), (1,)), ((), ())), preferred_element_type=jnp.float32
    )
    input_grad = lax.psum_scatter(
        (
            summed
            + lax.dot_general(
                value_flat,
                value_weight,
                (((1,), (1,)), ((), ())),
                preferred_element_type=jnp.float32,
            )
        ).astype(jnp.bfloat16),
        "tensor",
        scatter_dimension=0,
        tiled=True,
    )
    projected = jnp.dot(
        lax.all_gather(hidden_in, "tensor", axis=0, tiled=True),
        in_basis,
        preferred_element_type=jnp.float32,
    ).astype(jnp.bfloat16)
    key_part_proj = jnp.dot(key_flat, key_basis, preferred_element_type=jnp.float32)
    value_part_proj = jnp.dot(value_flat, value_basis, preferred_element_type=jnp.float32)
    docs_local = DOCS // tp_size
    key_proj, value_proj = (
        lax.psum(key_part_proj.astype(jnp.bfloat16), "tensor").astype(jnp.float32),
        lax.psum(value_part_proj.astype(jnp.bfloat16), "tensor").astype(jnp.float32),
    )
    weighted = spread_docs(doc_ids, tp_index * docs_local, docs_local, projected)
    key_docs = doc_outer(weighted, key_proj).reshape(docs_local, RANK, RANK)
    value_docs = doc_outer(weighted, value_proj).reshape(docs_local, RANK, RANK)
    return (input_grad, key_docs, value_docs)


def chip_at(place):
    place %= CHIPS
    return (place, 0) if place < CHIPS_Z else (CHIPS - 1 - place, 1)


def place_of(z, y):
    return z if y == 0 else CHIPS - 1 - z


def device(z, y, core, x):
    return ((z * CHIPS_Y + y) * CORES + core) * 2 + x


def pairs(move):
    out = []
    for z in range(CHIPS_Z):
        for y in range(CHIPS_Y):
            for core in range(CORES):
                for x in range(2):
                    out.append((device(z, y, core, x), device(*move(z, y, core, x))))
    return out


def send_x(a):
    return lax.ppermute(a, ("dp", "tensor"), pairs(lambda z, y, c, x: (z, y, c, 1 - x)))


def send_core(a):
    return lax.ppermute(a, ("dp", "tensor"), pairs(lambda z, y, c, x: (z, y, 1 - c, x)))


def send_ring(a, step):
    def move(z, y, c, x):
        to = chip_at(place_of(z, y) + step)
        return (to[0], to[1], c, x)

    return lax.ppermute(a, ("dp", "tensor"), pairs(move))


def attention_kernel(scal, start_ref, q_ref, do_ref, k_ref, v_ref, *refs):
    own_ref, send_ref, acck, accv = refs[-4:]
    tok = q_ref.shape[0]
    heads = q_ref.shape[1] // HD
    scale = HD ** (-0.5)
    c2 = scale * math.log2(math.e)
    acck[...] = jnp.zeros_like(acck)
    accv[...] = jnp.zeros_like(accv)
    nt = (((1,), (1,)), ((), ()))
    nn = (((1,), (0,)), ((), ()))
    f32 = jnp.float32
    wide = 3 * QB
    kpos = lax.broadcasted_iota(jnp.int32, (wide, QB), 0)
    qpos = lax.broadcasted_iota(jnp.int32, (wide, QB), 1)

    @pl.loop(0, tok // QB, unroll=4)
    def _(i):
        lo = jnp.maximum(i - 2, 0) * QB
        rows = pl.ds(pl.multiple_of(i * QB, QB), QB)
        window = pl.ds(pl.multiple_of(lo, QB), wide)
        keys = k_ref[window, :]
        vals = v_ref[window, :]
        ok = (kpos >= start_ref[:, rows] - lo) & (kpos - qpos <= i * QB - lo)
        bias = jnp.where(ok, 0.0, -1e30).astype(f32)
        bias = jnp.concatenate([bias] * heads, axis=1)
        cols = [slice(n * HD, (n + 1) * HD) for n in range(heads)]
        q = jnp.concatenate([q_ref[rows, c] for c in cols], axis=0)
        do = jnp.concatenate([do_ref[rows, c] for c in cols], axis=0)
        s = lax.dot_general(keys, q, nt, preferred_element_type=f32) + bias
        dp = lax.dot_general(vals, do, nt, preferred_element_type=f32)
        peak = jnp.max(s, axis=0, keepdims=True)
        e = jnp.exp2((s - peak) * c2)
        inv = 1.0 / jnp.sum(e, axis=0, keepdims=True)
        delta = jnp.sum(e * dp, axis=0, keepdims=True) * inv
        p = e * inv
        ds = (p * (dp - delta)).astype(jnp.bfloat16)
        accv[window, :] += lax.dot_general(
            p.astype(jnp.bfloat16), do, nn, preferred_element_type=f32
        )
        acck[window, :] += lax.dot_general(ds, q, nn, preferred_element_type=f32)

    half = tok // 2
    mine = pl.multiple_of(scal[X] * half, half)
    theirs = pl.multiple_of((1 - scal[X]) * half, half)
    for ref, start in ((own_ref, mine), (send_ref, theirs)):
        ref[:, :HD] = (acck[pl.ds(start, half), :] * scale).astype(jnp.bfloat16)
        ref[:, HD:] = accv[pl.ds(start, half), :].astype(jnp.bfloat16)


def attention(scal, start, queries, out_grad, keys, values, head, waits, before):
    tok = queries.shape[0]
    group = queries.shape[1] // keys.shape[1]
    wide = pl.BlockSpec((tok, group * HD), lambda g, s: (0, head))
    narrow = pl.BlockSpec((tok, HD), lambda g, s: (0, head))
    out = jax.ShapeDtypeStruct((tok // 2, 2 * PAIR * HD), jnp.bfloat16)
    out_spec = pl.BlockSpec((tok // 2, 2 * HD), lambda g, s: (0, head % PAIR))
    args = [start, queries, out_grad, keys, values, *waits, *before]
    return pl.pallas_call(
        attention_kernel,
        out_shape=(out, out),
        grid_spec=pltpu.PrefetchScalarGridSpec(
            num_scalar_prefetch=1,
            grid=(1,),
            in_specs=[pl.BlockSpec(start.shape, lambda g, s: (0, 0)), wide, wide, narrow, narrow]
            + [pl.BlockSpec(memory_space=pl.ANY)] * (len(args) - 5),
            out_specs=(out_spec, out_spec),
            scratch_shapes=[pltpu.VMEM((tok, HD), jnp.float32)] * 2,
        ),
        input_output_aliases={len(args) - 1 + n: n for n in range(len(before))},
        compiler_params=pltpu.CompilerParams(vmem_limit_bytes=ATT_VMEM),
        cost_estimate=COST,
        name="attention_back",
    )(scal, *args)


def docs_kernel(scal, doc_own, doc_oth, proj_own, proj_oth, kb, vb, *refs):
    heads = kb.shape[1] // HD
    owns, sends = refs[: heads // PAIR], refs[heads // PAIR : 2 * heads // PAIR]
    mine_ref, theirs_ref, total = refs[-3:]
    f32 = jnp.float32
    nt = (((1,), (1,)), ((), ()))
    nn = (((1,), (0,)), ((), ()))
    for first, (doc, proj, parts) in enumerate(((doc_own, proj_own, owns), (doc_oth, proj_oth, sends))):
        cut = lambda n: [r[:, a : a + HD] for r in parts for a in range(n * HD, r.shape[1], 2 * HD)]
        gk = jnp.concatenate(cut(0), axis=1)
        gv = jnp.concatenate(cut(1), axis=1)
        pk = lax.dot_general(gk, kb[...], nt, preferred_element_type=f32)
        pv = lax.dot_general(gv, vb[...], nt, preferred_element_type=f32)
        both = jnp.concatenate([pk, pv], axis=1)
        high = both.astype(jnp.bfloat16)
        low = (both - high.astype(f32)).astype(jnp.bfloat16)
        p = proj[...].astype(f32)
        ids = doc[...]
        w = jnp.concatenate(
            [jnp.where(ids == d, p, 0.0) for d in range(DOCS)], axis=0
        ).astype(jnp.bfloat16)
        add = lax.dot_general(w, high, nn, preferred_element_type=f32)
        add += lax.dot_general(w, low, nn, preferred_element_type=f32)
        if first == 0:
            total[...] = add
        else:
            total[...] += add
    half = total.shape[0] // 2
    mine_ref[...] = total[pl.ds(pl.multiple_of(scal[X] * half, half), half), :]
    theirs_ref[...] = total[pl.ds(pl.multiple_of((1 - scal[X]) * half, half), half), :]


def doc_sums(scal, doc_own, doc_oth, proj_own, proj_oth, kb, vb, owns, sends, waits):
    args = (doc_own, doc_oth, proj_own, proj_oth, kb, vb, *owns, *sends)
    rows = DOCS * RANK
    out = jax.ShapeDtypeStruct((rows // 2, 2 * RANK), jnp.float32)
    spec = lambda a: pl.BlockSpec(a.shape, lambda g, s: (0, 0))
    return pl.pallas_call(
        docs_kernel,
        out_shape=(out, out),
        grid_spec=pltpu.PrefetchScalarGridSpec(
            num_scalar_prefetch=1,
            grid=(1,),
            in_specs=[spec(a) for a in args] + [pl.BlockSpec(memory_space=pl.ANY)] * len(waits),
            out_specs=(spec(out), spec(out)),
            scratch_shapes=[pltpu.VMEM((rows, 2 * RANK), jnp.float32)],
        ),
        compiler_params=pltpu.CompilerParams(vmem_limit_bytes=VMEM),
        cost_estimate=COST,
        name="doc_sums",
    )(scal, *args, *waits)


def join_kernel(swap, scal, *refs):
    out = refs[-1]
    n = out.shape[1] // HD // 2
    k = n * HD
    for core in range(2 if swap else 1):

        @pl.when(scal[CORE] == core if swap else scal[CORE] >= 0)
        def _():
            for h in range(n):
                ref = refs[h // PAIR]
                for q in range(2):
                    at = (q ^ core) * k + h * HD
                    cols = slice((2 * (h % PAIR) + q) * HD, (2 * (h % PAIR) + q + 1) * HD)
                    out[:, at : at + HD] = ref[:, cols]


def join(scal, args, swap, waits):
    rows = args[0].shape[0]
    out = jax.ShapeDtypeStruct((rows, sum(a.shape[1] for a in args)), jnp.bfloat16)
    spec = lambda a: pl.BlockSpec(a.shape, lambda g, s: (0, 0))
    return pl.pallas_call(
        functools.partial(join_kernel, swap),
        out_shape=out,
        grid_spec=pltpu.PrefetchScalarGridSpec(
            num_scalar_prefetch=1,
            grid=(1,),
            in_specs=[spec(a) for a in args] + [pl.BlockSpec(memory_space=pl.ANY)] * len(waits),
            out_specs=spec(out),
        ),
        compiler_params=pltpu.CompilerParams(vmem_limit_bytes=VMEM),
        cost_estimate=COST,
        name="join",
    )(scal, *args, *waits)


def slabs_kernel(widths, places, counts, extra, scal, g_own, g_oth, wk, wv, *refs):
    n = len(widths)
    out, g, w, o, sem_g, sem_w, sem_o = refs[sum(counts) + extra :]
    k = wk.shape[1]
    total = sum(widths)
    begin = [sum(widths[:s]) for s in range(n)]
    load_g = [
        pltpu.make_async_copy(g_own, g.at[0], sem_g.at[0]),
        pltpu.make_async_copy(g_oth, g.at[1], sem_g.at[1]),
    ]
    for copy in load_g:
        copy.start()
    loads, stores = [], []
    for s in range(n):
        rows = pl.ds(pl.multiple_of(scal[places[s]], HD), widths[s])
        a, b = begin[s], begin[s] + widths[s]
        pieces = [(wk.at[rows, :], w.at[0, a:b]), (wv.at[rows, :], w.at[1, a:b])]
        these = refs[sum(counts[:s]) : sum(counts[: s + 1])]
        step = (b - a) // (counts[s] // 2)
        for q, ref in enumerate(these):
            to = a + q % (counts[s] // 2) * step
            pieces.append((ref, w.at[2 + q // (counts[s] // 2), to : to + step]))
        loads.append([pltpu.make_async_copy(c, d, sem_w.at[s, i]) for i, (c, d) in enumerate(pieces)])
        stores.append(pltpu.make_async_copy(o.at[:, a:b], out.at[:, rows], sem_o.at[s]))

    def begin_loads(s):
        for copy in loads[s]:
            copy.start()

    def end_loads(s):
        for copy in loads[s]:
            copy.wait()

    begin_loads(0)
    for copy in load_g:
        copy.wait()
    end_loads(0)
    if n > 1:
        begin_loads(1)
    cuts = [b // TILE for b in begin]

    @pl.loop(0, total // TILE)
    def _(t):
        for s in range(1, n):

            @pl.when(t == cuts[s])
            def _():
                end_loads(s)
                if s + 1 < n:
                    begin_loads(s + 1)

        rows = pl.ds(pl.multiple_of(t * TILE, TILE), TILE)
        o[:, rows] = sum(
            lax.dot_general(
                g[q // 2, :, q % 2 * k : (q % 2 + 1) * k],
                w[q, rows, :],
                (((1,), (1,)), ((), ())),
                preferred_element_type=jnp.float32,
            )
            for q in range(4)
        ).astype(jnp.bfloat16)
        for s in range(n - 1):

            @pl.when(t == (begin[s] + widths[s] - 1) // TILE)
            def _():
                stores[s].start()

    left = total % TILE
    if left:
        o[:, total - left :] = sum(
            lax.dot_general(
                g[q // 2, :, q % 2 * k : (q % 2 + 1) * k],
                w[q, total - left :, :],
                (((1,), (1,)), ((), ())),
                preferred_element_type=jnp.float32,
            )
            for q in range(4)
        ).astype(jnp.bfloat16)
    stores[-1].start()
    for copy in stores:
        copy.wait()


def slabs(scal, places, g, wk, wv, parts, waits, before=None):
    rows, depth = g[0].shape
    n = len(parts)
    counts = [len(part) for part in parts]
    widths = [sum(a.shape[0] for a in part) // 2 for part in parts]
    args = [*g, wk, wv] + [a for part in parts for a in part] + waits
    aliases = {}
    if before is not None:
        aliases = {len(args) + 1: 0}
        args.append(before)
    total = sum(widths)
    return pl.pallas_call(
        functools.partial(slabs_kernel, widths, places, counts, len(waits) + (before is not None)),
        out_shape=jax.ShapeDtypeStruct((rows, wk.shape[0]), jnp.bfloat16),
        grid_spec=pltpu.PrefetchScalarGridSpec(
            num_scalar_prefetch=1,
            grid=(1,),
            in_specs=[pl.BlockSpec(memory_space=pl.ANY)] * len(args),
            out_specs=pl.BlockSpec(memory_space=pl.ANY),
            scratch_shapes=[
                pltpu.VMEM((2, rows, depth), jnp.bfloat16),
                pltpu.VMEM((4, total, wk.shape[1]), jnp.bfloat16),
                pltpu.VMEM((rows, total), jnp.bfloat16),
                pltpu.SemaphoreType.DMA((2,)),
                pltpu.SemaphoreType.DMA((n, 6)),
                pltpu.SemaphoreType.DMA((n,)),
            ],
        ),
        input_output_aliases=aliases,
        compiler_params=pltpu.CompilerParams(vmem_limit_bytes=VMEM),
        cost_estimate=COST,
        name="slabs",
    )(scal, *args)


def pick_kernel(at, scal, wk, wv, *refs):
    out, sem = refs[-2:]
    size = out.shape[0]
    rows = pl.ds(pl.multiple_of(scal[at], 64), size)
    for core, ref in enumerate((wk, wv)):

        @pl.when(scal[CORE] == core)
        def _():
            copy = pltpu.make_async_copy(ref.at[rows, :], out, sem)
            copy.start()
            copy.wait()


def pick(scal, at, size, wk, wv, waits=()):
    spec = pl.BlockSpec(memory_space=pl.ANY)
    return pl.pallas_call(
        functools.partial(pick_kernel, at),
        out_shape=jax.ShapeDtypeStruct((size, wk.shape[1]), wk.dtype),
        grid_spec=pltpu.PrefetchScalarGridSpec(
            num_scalar_prefetch=1,
            grid=(1,),
            in_specs=[spec] * (2 + len(waits)),
            out_specs=pl.BlockSpec((size, wk.shape[1]), lambda g, s: (0, 0)),
            scratch_shapes=[pltpu.SemaphoreType.DMA],
        ),
        compiler_params=pltpu.CompilerParams(vmem_limit_bytes=VMEM),
        cost_estimate=COST,
        name="pick",
    )(scal, wk, wv, *waits)


def plane_body(
    hidden_in,
    queries,
    keys,
    values,
    out_grad,
    key_weight,
    value_weight,
    in_basis,
    key_basis,
    value_basis,
    doc_ids,
):
    tok = doc_ids.shape[0]
    half = tok // 2
    x = lax.axis_index("tensor")
    dp = lax.axis_index("dp")
    z, y, core = dp // (CHIPS_Y * CORES), (dp // CORES) % CHIPS_Y, dp % CORES
    place = jnp.where(y == 0, z, CHIPS - 1 - z)
    rows = key_weight.shape[0]
    slab = rows * 7 // 8 // CHIPS // HD * HD
    rest = rows - slab * CHIPS
    piece = slab // 2

    weights = (key_weight, value_weight)
    first = slab * CHIPS
    mine = place * slab
    starts = [(place + n) % CHIPS * slab for n in range(CHIPS)]
    scal = jnp.stack(
        [x, core, mine, mine + piece, first, *starts, first]
    ).astype(jnp.int32)
    sent = [pick(scal, SEND + n, piece, *weights) for n in range(2)]
    got = [send_x(a) for a in sent]
    both = lambda a: [*a, *[send_core(b) for b in a]]
    own_slab = both(got)
    up, down = got, got
    ups, downs = [up], [down]
    for _ in range(CHIPS // 2 - 1):
        up = [send_ring(a, 1) for a in up]
        down = [send_ring(a, -1) for a in down]
        ups.append(up)
        downs.append(down)
    far = [send_ring(up[0], 1), send_ring(down[1], -1)]
    stage = lambda n, half: [ups[n][half], downs[n][half]]

    docq = doc_ids[None, :]
    start = jnp.sum(doc_ids[None, :] < doc_ids[:, None], axis=1, dtype=jnp.int32)[None, :]
    proj = lax.dot_general(
        in_basis, hidden_in, (((0,), (1,)), ((), ())), preferred_element_type=jnp.float32
    ).astype(jnp.bfloat16)
    proj_oth = send_x(proj)
    heads = keys.shape[1] // HD
    rest_got = [send_x(pick(scal, REST, rest, *weights, got))]
    waits = [sent, got, stage(1, 0), stage(1, 1)]
    waits += [[]] * (heads - len(waits))
    owns, sends, others, last = [], [], [], []
    for head in range(heads):
        before = last if head % PAIR else []
        order = [] if head % PAIR else last[:1]
        last = list(
            attention(
                scal, start, queries, out_grad, keys, values, head, waits[head] + order, before
            )
        )
        if head % PAIR == PAIR - 1:
            owns.append(last[0])
            sends.append(last[1])
            others.append(send_x(last[1]))
    doc_own = lax.dynamic_slice_in_dim(docq, x * half, half, 1)
    doc_oth = lax.dynamic_slice_in_dim(docq, (1 - x) * half, half, 1)
    mine, theirs = doc_sums(
        scal, doc_own, doc_oth, proj, proj_oth, key_basis.T, value_basis.T, owns, sends, [*stage(2, 0), *rest_got]
    )
    docs = (mine + send_x(theirs)).reshape(DOCS // 2, RANK, 2 * RANK)

    g = [join(scal, owns, False, [*stage(2, 0), *stage(2, 1)]), join(scal, others, True, [])]
    ring = {0: own_slab, CHIPS // 2: both(far), None: both(rest_got)}
    for n in range(1, CHIPS // 2):
        ring[CHIPS - n], ring[n] = both(ups[n]), both(downs[n])
    out = None
    plan = (((0, 7, 1), []), ((6, 2, None), stage(3, 0)), ((5, 3), []), ((4,), []))
    for group, waits in plan:
        places = [SLABS + (CHIPS if n is None else n) for n in group]
        out = slabs(scal, places, g, *weights, [ring[n] for n in group], waits, out)
    return out, docs[:, :, :RANK], docs[:, :, RANK:]


def solution(mesh):
    placed = (
        P(("dp", "tensor"), None),
        P("dp", "tensor"),
        P("dp", "tensor"),
        P("dp", "tensor"),
        P("dp", "tensor"),
        P(None, "tensor"),
        P(None, "tensor"),
        P(),
        P("tensor", None),
        P("tensor", None),
        P("dp"),
    )
    fits = dict(mesh.shape) == {"dp": CHIPS * CORES, "tensor": 2}
    return jax.shard_map(
        plane_body if fits else general_body,
        mesh=mesh,
        in_specs=placed,
        out_specs=(
            P(("dp", "tensor"), None),
            P(("dp", "tensor"), None, None),
            P(("dp", "tensor"), None, None),
        ),
        check_vma=False,
    )
```

```python
import functools
import math

import jax
import jax.numpy as jnp
from jax import lax
from jax.experimental import pallas as pl
from jax.experimental.pallas import tpu as pltpu
from jax.sharding import PartitionSpec as P

HD = 128
RANK = 64
DOCS = 8
QB = 128
CHIPS_Z, CHIPS_Y, CORES = 4, 2, 2
CHIPS = CHIPS_Z * CHIPS_Y
MIB = 1 << 20
VMEM = 52 * MIB
ATT_VMEM = 52 * MIB
COST = pl.CostEstimate(flops=5 * 10**9, bytes_accessed=10**5, transcendentals=0)
PAIR = 2
TILE = 896
X, CORE, SEND, REST, SLABS = 0, 1, 2, 4, 5


def allowed_pairs(doc_ids):
    count = doc_ids.shape[0]
    position = jnp.arange(count, dtype=jnp.int32)
    same_doc = doc_ids[:, None] == doc_ids[None, :]
    return same_doc & (position[None, :] <= position[:, None])


def group_grads(query_heads, key_head, value_head, grad_heads, allowed):
    scale = HD ** (-0.5)

    def one_head(carry, operands):
        query, grad_out = operands
        scores = jnp.dot(query, key_head.T, preferred_element_type=jnp.float32) * scale
        scores = jnp.where(allowed, scores, -1e30)
        peak = jnp.max(scores, axis=1, keepdims=True)
        expo = jnp.exp(scores - peak)
        probs = expo / jnp.sum(expo, axis=1, keepdims=True)
        probs_low = probs.astype(jnp.bfloat16)
        value_step = lax.dot_general(
            probs_low, grad_out, (((0,), (0,)), ((), ())), preferred_element_type=jnp.float32
        )
        dprobs = jnp.dot(grad_out, value_head.T, preferred_element_type=jnp.float32)
        delta = jnp.sum(probs * dprobs, axis=1, keepdims=True)
        dscores = (probs * (dprobs - delta)).astype(jnp.bfloat16)
        key_step = (
            lax.dot_general(
                dscores, query, (((0,), (0,)), ((), ())), preferred_element_type=jnp.float32
            )
            * scale
        )
        return ((carry[0] + key_step, carry[1] + value_step), None)

    zeros = jnp.zeros((query_heads.shape[1], query_heads.shape[2]), jnp.float32)
    (key_sum, value_sum), _ = lax.scan(one_head, (zeros, zeros), (query_heads, grad_heads))
    return (key_sum.astype(jnp.bfloat16), value_sum.astype(jnp.bfloat16))


def doc_outer(weighted, grads):
    return lax.dot_general(
        weighted,
        grads,
        (((0,), (0,)), ((), ())),
        precision=lax.Precision.HIGHEST,
        preferred_element_type=jnp.float32,
    )


def spread_docs(doc_ids, doc_first, doc_count, projected):
    tok_count = doc_ids.shape[0]
    doc_range = doc_first + jnp.arange(doc_count, dtype=jnp.int32)
    onehot = (doc_ids[:, None] == doc_range[None, :]).astype(jnp.float32)
    return (onehot[:, :, None] * projected.astype(jnp.float32)[:, None, :]).reshape(
        tok_count, doc_count * RANK
    )


def general_body(
    hidden_in,
    queries,
    keys,
    values,
    out_grad,
    key_weight,
    value_weight,
    in_basis,
    key_basis,
    value_basis,
    doc_ids,
):
    tok_count = doc_ids.shape[0]
    tp_size = lax.axis_size("tensor")
    tp_index = lax.axis_index("tensor")
    local_kv = keys.shape[1] // HD
    local_q = queries.shape[1] // HD
    group = local_q // local_kv
    allowed = allowed_pairs(doc_ids)
    query_heads = queries.reshape(tok_count, local_kv, group, HD).transpose(1, 2, 0, 3)
    grad_heads = out_grad.reshape(tok_count, local_kv, group, HD).transpose(1, 2, 0, 3)
    key_heads = keys.reshape(tok_count, local_kv, HD).transpose(1, 0, 2)
    value_heads = values.reshape(tok_count, local_kv, HD).transpose(1, 0, 2)
    key_grad, value_grad = lax.map(
        lambda ops: group_grads(ops[0], ops[1], ops[2], ops[3], allowed),
        (query_heads, key_heads, value_heads, grad_heads),
    )
    key_flat = key_grad.transpose(1, 0, 2).reshape(tok_count, local_kv * HD)
    value_flat = value_grad.transpose(1, 0, 2).reshape(tok_count, local_kv * HD)
    summed = lax.dot_general(
        key_flat, key_weight, (((1,), (1,)), ((), ())), preferred_element_type=jnp.float32
    )
    input_grad = lax.psum_scatter(
        (
            summed
            + lax.dot_general(
                value_flat,
                value_weight,
                (((1,), (1,)), ((), ())),
                preferred_element_type=jnp.float32,
            )
        ).astype(jnp.bfloat16),
        "tensor",
        scatter_dimension=0,
        tiled=True,
    )
    projected = jnp.dot(
        lax.all_gather(hidden_in, "tensor", axis=0, tiled=True),
        in_basis,
        preferred_element_type=jnp.float32,
    ).astype(jnp.bfloat16)
    key_part_proj = jnp.dot(key_flat, key_basis, preferred_element_type=jnp.float32)
    value_part_proj = jnp.dot(value_flat, value_basis, preferred_element_type=jnp.float32)
    docs_local = DOCS // tp_size
    key_proj, value_proj = (
        lax.psum(key_part_proj.astype(jnp.bfloat16), "tensor").astype(jnp.float32),
        lax.psum(value_part_proj.astype(jnp.bfloat16), "tensor").astype(jnp.float32),
    )
    weighted = spread_docs(doc_ids, tp_index * docs_local, docs_local, projected)
    key_docs = doc_outer(weighted, key_proj).reshape(docs_local, RANK, RANK)
    value_docs = doc_outer(weighted, value_proj).reshape(docs_local, RANK, RANK)
    return (input_grad, key_docs, value_docs)


def chip_at(place):
    place %= CHIPS
    return (place, 0) if place < CHIPS_Z else (CHIPS - 1 - place, 1)


def place_of(z, y):
    return z if y == 0 else CHIPS - 1 - z


def device(z, y, core, x):
    return ((z * CHIPS_Y + y) * CORES + core) * 2 + x


def pairs(move):
    out = []
    for z in range(CHIPS_Z):
        for y in range(CHIPS_Y):
            for core in range(CORES):
                for x in range(2):
                    out.append((device(z, y, core, x), device(*move(z, y, core, x))))
    return out


def send_x(a):
    return lax.ppermute(a, ("dp", "tensor"), pairs(lambda z, y, c, x: (z, y, c, 1 - x)))


def send_core(a):
    return lax.ppermute(a, ("dp", "tensor"), pairs(lambda z, y, c, x: (z, y, 1 - c, x)))


def send_ring(a, step):
    def move(z, y, c, x):
        to = chip_at(place_of(z, y) + step)
        return (to[0], to[1], c, x)

    return lax.ppermute(a, ("dp", "tensor"), pairs(move))


def attention_kernel(scal, start_ref, q_ref, do_ref, k_ref, v_ref, *refs):
    own_ref, send_ref, acck, accv = refs[-4:]
    tok = q_ref.shape[0]
    heads = q_ref.shape[1] // HD
    scale = HD ** (-0.5)
    c2 = scale * math.log2(math.e)
    acck[...] = jnp.zeros_like(acck)
    accv[...] = jnp.zeros_like(accv)
    nt = (((1,), (1,)), ((), ()))
    nn = (((1,), (0,)), ((), ()))
    f32 = jnp.float32
    wide = 3 * QB
    kpos = lax.broadcasted_iota(jnp.int32, (wide, QB), 0)
    qpos = lax.broadcasted_iota(jnp.int32, (wide, QB), 1)

    @pl.loop(0, tok // QB, unroll=4)
    def _(i):
        lo = jnp.maximum(i - 2, 0) * QB
        rows = pl.ds(pl.multiple_of(i * QB, QB), QB)
        window = pl.ds(pl.multiple_of(lo, QB), wide)
        keys = k_ref[window, :]
        vals = v_ref[window, :]
        ok = (kpos >= start_ref[:, rows] - lo) & (kpos - qpos <= i * QB - lo)
        bias = jnp.where(ok, 0.0, -1e30).astype(f32)
        bias = jnp.concatenate([bias] * heads, axis=1)
        cols = [slice(n * HD, (n + 1) * HD) for n in range(heads)]
        q = jnp.concatenate([q_ref[rows, c] for c in cols], axis=0)
        do = jnp.concatenate([do_ref[rows, c] for c in cols], axis=0)
        s = lax.dot_general(keys, q, nt, preferred_element_type=f32) + bias
        dp = lax.dot_general(vals, do, nt, preferred_element_type=f32)
        peak = jnp.max(s, axis=0, keepdims=True)
        e = jnp.exp2((s - peak) * c2)
        inv = 1.0 / jnp.sum(e, axis=0, keepdims=True)
        delta = jnp.sum(e * dp, axis=0, keepdims=True) * inv
        p = e * inv
        ds = (p * (dp - delta)).astype(jnp.bfloat16)
        accv[window, :] += lax.dot_general(
            p.astype(jnp.bfloat16), do, nn, preferred_element_type=f32
        )
        acck[window, :] += lax.dot_general(ds, q, nn, preferred_element_type=f32)

    half = tok // 2
    mine = pl.multiple_of(scal[X] * half, half)
    theirs = pl.multiple_of((1 - scal[X]) * half, half)
    for ref, start in ((own_ref, mine), (send_ref, theirs)):
        ref[:, :HD] = (acck[pl.ds(start, half), :] * scale).astype(jnp.bfloat16)
        ref[:, HD:] = accv[pl.ds(start, half), :].astype(jnp.bfloat16)


def attention(scal, start, queries, out_grad, keys, values, head, waits, before):
    tok = queries.shape[0]
    group = queries.shape[1] // keys.shape[1]
    wide = pl.BlockSpec((tok, group * HD), lambda g, s: (0, head))
    narrow = pl.BlockSpec((tok, HD), lambda g, s: (0, head))
    out = jax.ShapeDtypeStruct((tok // 2, 2 * PAIR * HD), jnp.bfloat16)
    out_spec = pl.BlockSpec((tok // 2, 2 * HD), lambda g, s: (0, head % PAIR))
    args = [start, queries, out_grad, keys, values, *waits, *before]
    return pl.pallas_call(
        attention_kernel,
        out_shape=(out, out),
        grid_spec=pltpu.PrefetchScalarGridSpec(
            num_scalar_prefetch=1,
            grid=(1,),
            in_specs=[pl.BlockSpec(start.shape, lambda g, s: (0, 0)), wide, wide, narrow, narrow]
            + [pl.BlockSpec(memory_space=pl.ANY)] * (len(args) - 5),
            out_specs=(out_spec, out_spec),
            scratch_shapes=[pltpu.VMEM((tok, HD), jnp.float32)] * 2,
        ),
        input_output_aliases={len(args) - 1 + n: n for n in range(len(before))},
        compiler_params=pltpu.CompilerParams(vmem_limit_bytes=ATT_VMEM),
        cost_estimate=COST,
        name="attention_back",
    )(scal, *args)


def docs_kernel(scal, doc_own, doc_oth, proj_own, proj_oth, kb, vb, *refs):
    heads = kb.shape[1] // HD
    owns, sends = refs[: heads // PAIR], refs[heads // PAIR : 2 * heads // PAIR]
    mine_ref, theirs_ref, total = refs[-3:]
    f32 = jnp.float32
    nt = (((1,), (1,)), ((), ()))
    nn = (((1,), (0,)), ((), ()))
    for first, (doc, proj, parts) in enumerate(((doc_own, proj_own, owns), (doc_oth, proj_oth, sends))):
        cut = lambda n: [r[:, a : a + HD] for r in parts for a in range(n * HD, r.shape[1], 2 * HD)]
        gk = jnp.concatenate(cut(0), axis=1)
        gv = jnp.concatenate(cut(1), axis=1)
        pk = lax.dot_general(gk, kb[...], nt, preferred_element_type=f32)
        pv = lax.dot_general(gv, vb[...], nt, preferred_element_type=f32)
        both = jnp.concatenate([pk, pv], axis=1)
        high = both.astype(jnp.bfloat16)
        low = (both - high.astype(f32)).astype(jnp.bfloat16)
        p = proj[...].astype(f32)
        ids = doc[...]
        w = jnp.concatenate(
            [jnp.where(ids == d, p, 0.0) for d in range(DOCS)], axis=0
        ).astype(jnp.bfloat16)
        add = lax.dot_general(w, high, nn, preferred_element_type=f32)
        add += lax.dot_general(w, low, nn, preferred_element_type=f32)
        if first == 0:
            total[...] = add
        else:
            total[...] += add
    half = total.shape[0] // 2
    mine_ref[...] = total[pl.ds(pl.multiple_of(scal[X] * half, half), half), :]
    theirs_ref[...] = total[pl.ds(pl.multiple_of((1 - scal[X]) * half, half), half), :]


def doc_sums(scal, doc_own, doc_oth, proj_own, proj_oth, kb, vb, owns, sends, waits):
    args = (doc_own, doc_oth, proj_own, proj_oth, kb, vb, *owns, *sends)
    rows = DOCS * RANK
    out = jax.ShapeDtypeStruct((rows // 2, 2 * RANK), jnp.float32)
    spec = lambda a: pl.BlockSpec(a.shape, lambda g, s: (0, 0))
    return pl.pallas_call(
        docs_kernel,
        out_shape=(out, out),
        grid_spec=pltpu.PrefetchScalarGridSpec(
            num_scalar_prefetch=1,
            grid=(1,),
            in_specs=[spec(a) for a in args] + [pl.BlockSpec(memory_space=pl.ANY)] * len(waits),
            out_specs=(spec(out), spec(out)),
            scratch_shapes=[pltpu.VMEM((rows, 2 * RANK), jnp.float32)],
        ),
        compiler_params=pltpu.CompilerParams(vmem_limit_bytes=VMEM),
        cost_estimate=COST,
        name="doc_sums",
    )(scal, *args, *waits)


def join_kernel(swap, scal, *refs):
    out = refs[-1]
    n = out.shape[1] // HD // 2
    k = n * HD
    for core in range(2 if swap else 1):

        @pl.when(scal[CORE] == core if swap else scal[CORE] >= 0)
        def _():
            for h in range(n):
                ref = refs[h // PAIR]
                for q in range(2):
                    at = (q ^ core) * k + h * HD
                    cols = slice((2 * (h % PAIR) + q) * HD, (2 * (h % PAIR) + q + 1) * HD)
                    out[:, at : at + HD] = ref[:, cols]


def join(scal, args, swap, waits):
    rows = args[0].shape[0]
    out = jax.ShapeDtypeStruct((rows, sum(a.shape[1] for a in args)), jnp.bfloat16)
    spec = lambda a: pl.BlockSpec(a.shape, lambda g, s: (0, 0))
    return pl.pallas_call(
        functools.partial(join_kernel, swap),
        out_shape=out,
        grid_spec=pltpu.PrefetchScalarGridSpec(
            num_scalar_prefetch=1,
            grid=(1,),
            in_specs=[spec(a) for a in args] + [pl.BlockSpec(memory_space=pl.ANY)] * len(waits),
            out_specs=spec(out),
        ),
        compiler_params=pltpu.CompilerParams(vmem_limit_bytes=VMEM),
        cost_estimate=COST,
        name="join",
    )(scal, *args, *waits)


def slabs_kernel(widths, places, counts, extra, scal, g_own, g_oth, wk, wv, *refs):
    n = len(widths)
    out, g, w, o, sem_g, sem_w, sem_o = refs[sum(counts) + extra :]
    k = wk.shape[1]
    total = sum(widths)
    begin = [sum(widths[:s]) for s in range(n)]
    load_g = [
        pltpu.make_async_copy(g_own, g.at[0], sem_g.at[0]),
        pltpu.make_async_copy(g_oth, g.at[1], sem_g.at[1]),
    ]
    for copy in load_g:
        copy.start()
    loads, stores = [], []
    for s in range(n):
        rows = pl.ds(pl.multiple_of(scal[places[s]], HD), widths[s])
        a, b = begin[s], begin[s] + widths[s]
        pieces = [(wk.at[rows, :], w.at[0, a:b]), (wv.at[rows, :], w.at[1, a:b])]
        these = refs[sum(counts[:s]) : sum(counts[: s + 1])]
        step = (b - a) // (counts[s] // 2)
        for q, ref in enumerate(these):
            to = a + q % (counts[s] // 2) * step
            pieces.append((ref, w.at[2 + q // (counts[s] // 2), to : to + step]))
        loads.append([pltpu.make_async_copy(c, d, sem_w.at[s, i]) for i, (c, d) in enumerate(pieces)])
        stores.append(pltpu.make_async_copy(o.at[:, a:b], out.at[:, rows], sem_o.at[s]))

    def begin_loads(s):
        for copy in loads[s]:
            copy.start()

    def end_loads(s):
        for copy in loads[s]:
            copy.wait()

    begin_loads(0)
    for copy in load_g:
        copy.wait()
    end_loads(0)
    if n > 1:
        begin_loads(1)
    cuts = [b // TILE for b in begin]

    @pl.loop(0, total // TILE)
    def _(t):
        for s in range(1, n):

            @pl.when(t == cuts[s])
            def _():
                end_loads(s)
                if s + 1 < n:
                    begin_loads(s + 1)

        rows = pl.ds(pl.multiple_of(t * TILE, TILE), TILE)
        o[:, rows] = sum(
            lax.dot_general(
                g[q // 2, :, q % 2 * k : (q % 2 + 1) * k],
                w[q, rows, :],
                (((1,), (1,)), ((), ())),
                preferred_element_type=jnp.float32,
            )
            for q in range(4)
        ).astype(jnp.bfloat16)
        for s in range(n - 1):

            @pl.when(t == (begin[s] + widths[s] - 1) // TILE)
            def _():
                stores[s].start()

    left = total % TILE
    if left:
        o[:, total - left :] = sum(
            lax.dot_general(
                g[q // 2, :, q % 2 * k : (q % 2 + 1) * k],
                w[q, total - left :, :],
                (((1,), (1,)), ((), ())),
                preferred_element_type=jnp.float32,
            )
            for q in range(4)
        ).astype(jnp.bfloat16)
    stores[-1].start()
    for copy in stores:
        copy.wait()


def slabs(scal, places, g, wk, wv, parts, waits, before=None):
    rows, depth = g[0].shape
    n = len(parts)
    counts = [len(part) for part in parts]
    widths = [sum(a.shape[0] for a in part) // 2 for part in parts]
    args = [*g, wk, wv] + [a for part in parts for a in part] + waits
    aliases = {}
    if before is not None:
        aliases = {len(args) + 1: 0}
        args.append(before)
    total = sum(widths)
    return pl.pallas_call(
        functools.partial(slabs_kernel, widths, places, counts, len(waits) + (before is not None)),
        out_shape=jax.ShapeDtypeStruct((rows, wk.shape[0]), jnp.bfloat16),
        grid_spec=pltpu.PrefetchScalarGridSpec(
            num_scalar_prefetch=1,
            grid=(1,),
            in_specs=[pl.BlockSpec(memory_space=pl.ANY)] * len(args),
            out_specs=pl.BlockSpec(memory_space=pl.ANY),
            scratch_shapes=[
                pltpu.VMEM((2, rows, depth), jnp.bfloat16),
                pltpu.VMEM((4, total, wk.shape[1]), jnp.bfloat16),
                pltpu.VMEM((rows, total), jnp.bfloat16),
                pltpu.SemaphoreType.DMA((2,)),
                pltpu.SemaphoreType.DMA((n, 6)),
                pltpu.SemaphoreType.DMA((n,)),
            ],
        ),
        input_output_aliases=aliases,
        compiler_params=pltpu.CompilerParams(vmem_limit_bytes=VMEM),
        cost_estimate=COST,
        name="slabs",
    )(scal, *args)


def pick_kernel(at, scal, wk, wv, *refs):
    out, sem = refs[-2:]
    size = out.shape[0]
    rows = pl.ds(pl.multiple_of(scal[at], 64), size)
    for core, ref in enumerate((wk, wv)):

        @pl.when(scal[CORE] == core)
        def _():
            copy = pltpu.make_async_copy(ref.at[rows, :], out, sem)
            copy.start()
            copy.wait()


def pick(scal, at, size, wk, wv, waits=()):
    spec = pl.BlockSpec(memory_space=pl.ANY)
    return pl.pallas_call(
        functools.partial(pick_kernel, at),
        out_shape=jax.ShapeDtypeStruct((size, wk.shape[1]), wk.dtype),
        grid_spec=pltpu.PrefetchScalarGridSpec(
            num_scalar_prefetch=1,
            grid=(1,),
            in_specs=[spec] * (2 + len(waits)),
            out_specs=pl.BlockSpec((size, wk.shape[1]), lambda g, s: (0, 0)),
            scratch_shapes=[pltpu.SemaphoreType.DMA],
        ),
        compiler_params=pltpu.CompilerParams(vmem_limit_bytes=VMEM),
        cost_estimate=COST,
        name="pick",
    )(scal, wk, wv, *waits)


def plane_body(
    hidden_in,
    queries,
    keys,
    values,
    out_grad,
    key_weight,
    value_weight,
    in_basis,
    key_basis,
    value_basis,
    doc_ids,
):
    tok = doc_ids.shape[0]
    half = tok // 2
    x = lax.axis_index("tensor")
    dp = lax.axis_index("dp")
    z, y, core = dp // (CHIPS_Y * CORES), (dp // CORES) % CHIPS_Y, dp % CORES
    place = jnp.where(y == 0, z, CHIPS - 1 - z)
    rows = key_weight.shape[0]
    slab = rows * 7 // 8 // CHIPS // HD * HD
    rest = rows - slab * CHIPS
    piece = slab // 2

    weights = (key_weight, value_weight)
    first = slab * CHIPS
    mine = place * slab
    starts = [(place + n) % CHIPS * slab for n in range(CHIPS)]
    scal = jnp.stack(
        [x, core, mine, mine + piece, first, *starts, first]
    ).astype(jnp.int32)
    sent = [pick(scal, SEND + n, piece, *weights) for n in range(2)]
    got = [send_x(a) for a in sent]
    both = lambda a: [*a, *[send_core(b) for b in a]]
    own_slab = both(got)
    up, down = got, got
    ups, downs = [up], [down]
    for _ in range(CHIPS // 2 - 1):
        up = [send_ring(a, 1) for a in up]
        down = [send_ring(a, -1) for a in down]
        ups.append(up)
        downs.append(down)
    far = [send_ring(up[0], 1), send_ring(down[1], -1)]
    stage = lambda n, half: [ups[n][half], downs[n][half]]

    docq = doc_ids[None, :]
    start = jnp.sum(doc_ids[None, :] < doc_ids[:, None], axis=1, dtype=jnp.int32)[None, :]
    proj = lax.dot_general(
        in_basis, hidden_in, (((0,), (1,)), ((), ())), preferred_element_type=jnp.float32
    ).astype(jnp.bfloat16)
    proj_oth = send_x(proj)
    heads = keys.shape[1] // HD
    rest_got = [send_x(pick(scal, REST, rest, *weights, got))]
    waits = [sent, got, stage(1, 0), stage(1, 1)]
    waits += [[]] * (heads - len(waits))
    owns, sends, others, last = [], [], [], []
    for head in range(heads):
        before = last if head % PAIR else []
        order = [] if head % PAIR else last[:1]
        last = list(
            attention(
                scal, start, queries, out_grad, keys, values, head, waits[head] + order, before
            )
        )
        if head % PAIR == PAIR - 1:
            owns.append(last[0])
            sends.append(last[1])
            others.append(send_x(last[1]))
    doc_own = lax.dynamic_slice_in_dim(docq, x * half, half, 1)
    doc_oth = lax.dynamic_slice_in_dim(docq, (1 - x) * half, half, 1)
    mine, theirs = doc_sums(
        scal, doc_own, doc_oth, proj, proj_oth, key_basis.T, value_basis.T, owns, sends, rest_got
    )
    docs = (mine + send_x(theirs)).reshape(DOCS // 2, RANK, 2 * RANK)

    g = [join(scal, owns, False, [*stage(2, 0), *stage(2, 1)]), join(scal, others, True, [])]
    ring = {0: own_slab, CHIPS // 2: both(far), None: both(rest_got)}
    for n in range(1, CHIPS // 2):
        ring[CHIPS - n], ring[n] = both(ups[n]), both(downs[n])
    out = None
    plan = (((0, 7, 1), []), ((6, 2, None), stage(3, 0)), ((5, 3), []), ((4,), []))
    for group, waits in plan:
        places = [SLABS + (CHIPS if n is None else n) for n in group]
        out = slabs(scal, places, g, *weights, [ring[n] for n in group], waits, out)
    return out, docs[:, :, :RANK], docs[:, :, RANK:]


def solution(mesh):
    placed = (
        P(("dp", "tensor"), None),
        P("dp", "tensor"),
        P("dp", "tensor"),
        P("dp", "tensor"),
        P("dp", "tensor"),
        P(None, "tensor"),
        P(None, "tensor"),
        P(),
        P("tensor", None),
        P("tensor", None),
        P("dp"),
    )
    fits = dict(mesh.shape) == {"dp": CHIPS * CORES, "tensor": 2}
    return jax.shard_map(
        plane_body if fits else general_body,
        mesh=mesh,
        in_specs=placed,
        out_specs=(
            P(("dp", "tensor"), None),
            P(("dp", "tensor"), None, None),
            P(("dp", "tensor"), None, None),
        ),
        check_vma=False,
    )
```
